32 devices in a mesh: groups: 2 (over x), gx: 16 (over z, y, core).
Axes of the slice: x: 2, y: 2, z: 4, core: 2. Of those that a mesh axis runs over, the one named last changes fastest.
Arguments:
- node_feat: bfloat16 [3200, 4096], P(None, ('groups', 'gx')), parts along dimension 1, may hold values from -6 to 6
- frames: bfloat16 [115, 16384], P(None, ('groups', 'gx')), parts along dimension 1, may hold values from -2.390625 to 2.390625
- neighbours: int32 [4, 4096], P(None, ('groups', 'gx')), parts along dimension 1, may hold values from 0 to 2047, as said below
- counts: int32 [4096], P(('groups', 'gx')), parts along dimension 0, may hold values from 2 to 4, as said below
- positions: float32 [3, 4096], P(None, ('groups', 'gx')), parts along dimension 1, may hold values from 0 to 331.776, as said below
- velocities: float32 [3, 4096], P(None, ('groups', 'gx')), parts along dimension 1
- masses: float32 [4096], P(('groups', 'gx')), parts along dimension 0, may hold values from 1 to 2
- thermal_noise: float32 [3, 4096], P(None, ('groups', 'gx')), parts along dimension 1, may hold values from -6 to 6
- box_lengths: float32 [6], P('groups'), parts along dimension 0, may hold values from 6.5 to 331.776
- control: float32 [6], P('groups'), parts along dimension 0, may hold values from 0.05 to 2
- conv_weight: bfloat16 [2, 5, 128, 128], replicated, may hold values from -0.5 to 0.5
- radial_weight: float32 [2, 16, 128], replicated, may hold values from -3 to 3
- readout: float32 [5, 128], replicated, may hold values from -0.5 to 0.5
Outputs:
- fractional: float32 [3, 4096], P(None, ('groups', 'gx')), parts along dimension 1
- new_velocities: float32 [3, 4096], P(None, ('groups', 'gx')), parts along dimension 1
- new_box: float32 [6], P('groups'), parts along dimension 0
The draws below stay inside these ranges and needn't reach their ends.
There are 2 independent parts, one for each index of `groups`. The reference program is written for one: setup_inputs(seed, part) draws one part's arguments, and reference() takes and returns one part's arrays. A program takes and returns all parts, laid end to end along the dimension named above; an argument that names none is the same for every part. Nothing has to cross between parts.
Inputs may be any that keep to these rules, and one draw needn't show every extreme that they name: `neighbours`: the 4 slots of an atom name different atoms other than itself, each at most 32 places away from it in the cyclic order of atoms. `counts`: slots at or past an atom's count are padding. `positions`: every atom lies inside the box.
All inputs are finite; a program needn't handle non-finite values.
Results may differ from the reference program's by a relative error of at most 0.0055.
Values may be sent and summed in bfloat16 or wider, within the bound.
No kernel may reach another device: no remote copies, remote signals or barrier semaphores. Data moves between devices by JAX's collectives and lax.ppermute only.
A program may use at most 128 MiB of HBM per device.

```python
import math
import jax
import jax.numpy as jnp
from jax import lax

C = 128
LMAX = 4
MMAX = 2
NCOEF = 25
WROWS = 115
KNB = 4
GHOST = 32
NRBF = 16
LAYERS = 2
ATOMS = 2048


def slab_geometry(key):
    key_box = jax.random.fold_in(key, 101)
    key_pos = jax.random.fold_in(key, 102)
    sides = jax.random.uniform(key_box, (2,), jnp.float32, 6.5, 7.5)
    stretch = jax.random.uniform(jax.random.fold_in(key_box, 1), (), jnp.float32, 0.98, 1.0)
    length = ATOMS * 0.16 * stretch
    box_lengths = jnp.concatenate([length[None], sides])
    jitter = jax.random.uniform(key_pos, (3, ATOMS), jnp.float32, 0.0, 1.0)
    along = (jnp.arange(ATOMS, dtype=jnp.float32) + jitter[0]) / ATOMS * length
    placed = jnp.stack([along, jitter[1] * sides[0], jitter[2] * sides[1]])
    return (box_lengths, placed)


def draw_box_lengths(key, part):
    box_lengths, placed = slab_geometry(key)
    return box_lengths


def draw_positions(key, part):
    box_lengths, placed = slab_geometry(key)
    return placed


def draw_neighbours(key, part):
    key = jax.random.fold_in(key, 3)
    scores = jax.random.randint(key, (ATOMS, 2 * GHOST), 0, 1 << 20)
    scores = scores * (2 * GHOST) + jnp.arange(2 * GHOST, dtype=jnp.int32)[None, :]
    chosen = jnp.argsort(scores, axis=1, stable=True)[:, :KNB]
    offsets = jnp.where(chosen < GHOST, chosen - GHOST, chosen - GHOST + 1)
    index = jnp.mod(jnp.arange(ATOMS, dtype=jnp.int32)[:, None] + offsets, ATOMS)
    return index.T.astype(jnp.int32)


def draw_counts(key, part):
    key = jax.random.fold_in(key, 4)
    drawn = jax.random.randint(key, (ATOMS,), KNB // 2, KNB + 1)
    return drawn.at[0].set(KNB).at[1].set(KNB // 2).astype(jnp.int32)


def draw_velocities(key, part):
    key = jax.random.fold_in(key, 5)
    along = jnp.arange(ATOMS, dtype=jnp.float32)[None, :] / ATOMS
    return jnp.sqrt(1.0 + 2.0 * along) * jax.random.normal(key, (3, ATOMS), jnp.float32)


def draw_control(key, part):
    key = jax.random.fold_in(key, 7)
    noise_seed_list = jax.random.split(key, 3)
    thermostat_kelvin_setpoint = jnp.exp(jax.random.uniform(noise_seed_list[0], (1,), jnp.float32, -0.6931472, 0.6931472))
    barostat_relaxation_factor = jax.random.uniform(noise_seed_list[1], (1,), jnp.float32, 1.0, 2.0)
    desired_stress_level = jax.random.uniform(noise_seed_list[2], (1,), jnp.float32, 0.05, 0.3)
    return jnp.concatenate([thermostat_kelvin_setpoint, barostat_relaxation_factor, desired_stress_level])


def block_scale(rng, shape, shards, low, high):
    gain = 1.0
    for axis_at, shards_of in shards:
        heights = jax.random.uniform(jax.random.fold_in(jax.random.fold_in(rng, 6), axis_at), (shards_of,), jnp.float32, low / len(shards), high / len(shards))
        gain = gain * jnp.repeat(jnp.exp(heights), shape[axis_at] // shards_of).reshape((-1,) + (1,) * (len(shape) - 1 - axis_at))
    return gain


def bell_draw(stream_key, dims, spread, most, cuts=(), held_as=jnp.bfloat16):
    result = jax.random.normal(stream_key, dims, jnp.float32) * spread
    if len(cuts) > 0:
        result = block_scale(stream_key, dims, cuts, -0.22, 0.18) * result
    return jnp.clip(result, min=-most, max=most).astype(held_as)


def setup_inputs(seed: int = 0, part: int = 0) -> dict:
    key_of = jax.random.split(jax.random.key(seed), 14)
    part_keys = jax.random.split(jax.random.fold_in(key_of[13], part), 14)
    node_feat = bell_draw(part_keys[0], (NCOEF * C, ATOMS), 1.0, 6.0, ((1, 16),))
    frames = bell_draw(part_keys[1], (WROWS, ATOMS * KNB), 0.4, 2.390625, ((1, 16),))
    neighbours = draw_neighbours(jax.random.fold_in(jax.random.fold_in(key_of[13], part), 71), part)
    counts = draw_counts(jax.random.fold_in(jax.random.fold_in(key_of[13], part), 71), part)
    positions = draw_positions(jax.random.fold_in(jax.random.fold_in(key_of[13], part), 71), part)
    velocities = draw_velocities(jax.random.fold_in(jax.random.fold_in(key_of[13], part), 71), part)
    masses = jnp.clip(jnp.exp(math.log(2.0) - 0.6931472 * jax.random.uniform(part_keys[6], (ATOMS,), jnp.float32) ** block_scale(part_keys[6], (ATOMS,), ((0, 16),), -0.2, 0.2)), 1.0, 2.0)
    thermal_noise = bell_draw(part_keys[7], (3, ATOMS), 1.0, 6.0, ((1, 16),), jnp.float32)
    box_lengths = draw_box_lengths(jax.random.fold_in(jax.random.fold_in(key_of[13], part), 71), part)
    control = draw_control(jax.random.fold_in(jax.random.fold_in(key_of[13], part), 71), part)
    conv_weight = bell_draw(key_of[10], (LAYERS, 2 * MMAX + 1, C, C), C ** -0.5, 0.5)
    radial_weight = bell_draw(key_of[11], (LAYERS, NRBF, C), 0.6, 3.0, (), jnp.float32)
    readout = bell_draw(key_of[12], (LMAX + 1, C), C ** -0.5, 0.5, (), jnp.float32)
    return dict(node_feat=node_feat, frames=frames, neighbours=neighbours, counts=counts, positions=positions, velocities=velocities, masses=masses, thermal_noise=thermal_noise, box_lengths=box_lengths, control=control, conv_weight=conv_weight, radial_weight=radial_weight, readout=readout)


EPSILON = 1e-06
SOFTENING = 0.25
STEP_TIME = 0.1
FRICTION = 0.9
RADIAL_SPREAD = 0.5

def frame_layout():
    layout = []
    offset = 0
    for degree in range(LMAX + 1):
        row_count = min(2 * degree + 1, 2 * MMAX + 1)
        layout.append((degree, row_count, offset))
        offset = offset + row_count * (2 * degree + 1)
    return layout

def keep_round(values):
    rounded = lax.optimization_barrier(values.astype(jnp.bfloat16)).astype(jnp.float32)
    return values + lax.stop_gradient(rounded - values)

def contract(closed_expression, former, latter):
    return jnp.einsum(closed_expression, former.astype(jnp.float32), latter.astype(jnp.float32))

def edge_messages(source, source_pos, target_pos, source_index, slot_mask, frames, conv_weights, radial_weights):
    channels = source.shape[0] // NCOEF
    edge_total = source_index.shape[0]
    targets = target_pos.shape[1]
    squares = lax.optimization_barrier(jnp.mean(source * source, axis=0, keepdims=True))
    normed = source * lax.rsqrt(squares + EPSILON)
    picked = jnp.take(normed, source_index, axis=1).astype(jnp.bfloat16).reshape(NCOEF, channels, edge_total)
    vectors = jnp.take(source_pos, source_index, axis=1) - jnp.repeat(target_pos, KNB, axis=1)
    distance = jnp.sqrt(lax.optimization_barrier(jnp.sum(vectors * vectors, axis=0)) + SOFTENING)
    centers = 0.5 + 5.5 * jnp.arange(NRBF, dtype=jnp.float32)[:, None] / (NRBF - 1)
    radial_basis = jnp.exp(-jnp.square((distance[None, :] - centers) / RADIAL_SPREAD))
    edge_gates = jnp.dot(radial_weights.T, radial_basis, precision=lax.Precision.HIGHEST)
    layout = frame_layout()
    in_frame = []
    frame_blocks = []
    for degree, row_count, offset in layout:
        degree_size = 2 * degree + 1
        frame_block = frames[offset:offset + row_count * degree_size].reshape(row_count, degree_size, edge_total)
        frame_blocks.append(frame_block)
        first_row = degree * degree
        rotated = contract('rke,kce->rce', frame_block, picked[first_row:first_row + degree_size])
        in_frame.append(rotated.astype(jnp.bfloat16))
    out_rows = [[None] * row_count for degree, row_count, offset in layout]
    zero_order = jnp.stack([rotated[0] for rotated in in_frame])
    zero_out = contract('rce,cd->rde', zero_order, conv_weights[0])
    for degree in range(LMAX + 1):
        out_rows[degree][0] = zero_out[degree]
    for azimuth in range(1, MMAX + 1):
        members = list(range(azimuth, LMAX + 1))
        plus_rows = jnp.stack([in_frame[degree][2 * azimuth - 1] for degree in members])
        minus_rows = jnp.stack([in_frame[degree][2 * azimuth] for degree in members])
        real_weight = conv_weights[2 * azimuth - 1]
        imag_weight = conv_weights[2 * azimuth]
        plus_out = contract('rce,cd->rde', plus_rows, real_weight) - contract('rce,cd->rde', minus_rows, imag_weight)
        minus_out = contract('rce,cd->rde', minus_rows, real_weight) + contract('rce,cd->rde', plus_rows, imag_weight)
        for member_index, degree in enumerate(members):
            out_rows[degree][2 * azimuth - 1] = plus_out[member_index]
            out_rows[degree][2 * azimuth] = minus_out[member_index]
    rotated_back = []
    for degree, row_count, offset in layout:
        gated_rows = (jnp.stack(out_rows[degree]) * edge_gates[None]).astype(jnp.bfloat16)
        rotated_back.append(contract('rke,rce->kce', frame_blocks[degree], gated_rows))
    message = jnp.concatenate(rotated_back, axis=0).reshape(NCOEF, channels, targets, KNB)
    return lax.optimization_barrier(jnp.sum(message * slot_mask[None, None], axis=3)).reshape(NCOEF * channels, targets)

def layer_block(window_feat, window_pos, source_index, slot_mask, frames, conv_weights, radial_weights):
    message = edge_messages(window_feat, window_pos, window_pos[:, GHOST:2 * GHOST], source_index, slot_mask, frames, conv_weights, radial_weights)
    return window_feat[:, GHOST:2 * GHOST] + message * KNB ** (-0.5)

def readout_energy(hidden, readout):
    channels = hidden.shape[0] // NCOEF
    shaped = hidden.reshape(NCOEF, channels, hidden.shape[1])
    energy = jnp.zeros((), jnp.float32)
    for degree in range(LMAX + 1):
        degree_rows = shaped[degree * degree:(degree + 1) * (degree + 1)]
        energy = energy + jnp.sum(readout[degree][:, None] * lax.optimization_barrier(jnp.mean(degree_rows * degree_rows, axis=0)))
    return energy

def block_inputs(extended_index, live_slots, frames, block_index):
    start_col = block_index * GHOST
    local_index = jnp.mod(lax.dynamic_slice_in_dim(extended_index, start_col, GHOST, 1) - start_col, ATOMS).astype(jnp.int32)
    source_index = local_index.T.reshape(-1)
    slot_mask = lax.dynamic_slice_in_dim(live_slots, start_col, GHOST, 1).T
    frame_cols = lax.dynamic_slice_in_dim(frames, start_col * KNB, GHOST * KNB, 1)
    return (source_index, slot_mask, frame_cols)

def split_window(values):
    return jnp.moveaxis(values.reshape(values.shape[0], 3, GHOST), 1, 0)

def fold_cyclic(pieces):
    summed = jnp.zeros((pieces.shape[2], ATOMS), jnp.float32)
    for third_part in range(3):
        arranged_frame_grid = jnp.moveaxis(pieces[:, third_part], 0, 1).reshape(pieces.shape[2], ATOMS)
        summed = summed + jnp.roll(arranged_frame_grid, (third_part - 1) * GHOST, axis=1)
    return summed

def cyclic_pad(values, box_shift):
    return jnp.concatenate([values[:, ATOMS - GHOST:] - box_shift, values, values[:, :GHOST] + box_shift], axis=1)

def reference(node_feat, frames, neighbours, counts, positions, velocities, masses, thermal_noise, box_lengths, control, conv_weight, radial_weight, readout):
    block_total = ATOMS // GHOST
    feat_rows = node_feat.shape[0]
    nothing = jnp.zeros((), jnp.float32)
    box_shift = jnp.stack([box_lengths[0], nothing, nothing])[:, None]
    pos_pad = cyclic_pad(positions, box_shift)
    feat_pad = cyclic_pad(node_feat.astype(jnp.float32), nothing)
    live_slots = (jnp.arange(KNB, dtype=jnp.int32)[:, None] < counts[None, :]).astype(jnp.float32)
    extended_index = jnp.mod(neighbours + GHOST, ATOMS).astype(jnp.int32)
    block_ids = jnp.arange(block_total, dtype=jnp.int32)

    def windowed(values, block_index):
        return lax.dynamic_slice_in_dim(values, block_index * GHOST, 3 * GHOST, 1)

    def relative(pos_window):
        return pos_window - pos_window[:, GHOST:GHOST + 1]

    def first_layer(block_index, pos_window):
        source_index, slot_mask, frame_cols = block_inputs(extended_index, live_slots, frames, block_index)
        return keep_round(layer_block(windowed(feat_pad, block_index), pos_window, source_index, slot_mask, frame_cols, conv_weight[0], radial_weight[0]))

    def forward_block(block_index):
        return first_layer(block_index, windowed(pos_pad, block_index))
    hidden = lax.map(forward_block, block_ids)
    hidden = jnp.moveaxis(hidden, 0, 1).reshape(feat_rows, ATOMS)
    hidden_pad = cyclic_pad(hidden, nothing)

    def second_block(block_index):
        source_index, slot_mask, frame_cols = block_inputs(extended_index, live_slots, frames, block_index)
        pos_window = windowed(pos_pad, block_index)

        def energy_of(feat_window, pos_in):
            upper_feat = layer_block(feat_window, pos_in, source_index, slot_mask, frame_cols, conv_weight[1], radial_weight[1])
            return readout_energy(upper_feat, readout)
        energy_value, pullback = jax.vjp(energy_of, windowed(hidden_pad, block_index), pos_window)
        feat_grad, pos_grad = pullback(jnp.ones((), jnp.float32))
        return (split_window(feat_grad), split_window(pos_grad), -jnp.sum(relative(pos_window) * pos_grad))
    feat_pieces, pos_pieces_two, virial_two = lax.map(second_block, block_ids)
    hidden_grad = fold_cyclic(feat_pieces)

    def first_back(block_index):
        pos_window = windowed(pos_pad, block_index)
        layer_value, pullback = jax.vjp(lambda pos_in: first_layer(block_index, pos_in), pos_window)
        pos_grad, = pullback(lax.dynamic_slice_in_dim(hidden_grad, block_index * GHOST, GHOST, 1))
        return (split_window(pos_grad), -jnp.sum(relative(pos_window) * pos_grad))
    pos_pieces_one, virial_one = lax.map(first_back, block_ids)
    forces = -(fold_cyclic(pos_pieces_one) + fold_cyclic(pos_pieces_two))
    virial = jnp.sum(virial_one) + jnp.sum(virial_two)
    kicked = velocities + STEP_TIME * forces / masses[None, :]
    kinetic = 0.5 * jnp.sum(masses * lax.optimization_barrier(jnp.sum(kicked * kicked, axis=0)))
    volume = box_lengths[0] * box_lengths[1] * box_lengths[2]
    pressure = (2.0 * kinetic + virial) / (3.0 * volume)
    thermal = FRICTION * kicked + jnp.sqrt((1.0 - FRICTION * FRICTION) * control[0] / masses)[None, :] * thermal_noise
    rescale = jnp.exp(control[1] * (pressure - control[2]) / 3.0)
    fractional = (positions + STEP_TIME * thermal) / box_lengths[:, None]
    return (fractional, thermal / rescale, box_lengths * rescale)
```

```python
import functools

import jax
import jax.numpy as jnp
from jax import lax
from jax.experimental import pallas as pl
from jax.experimental.pallas import tpu as pltpu
from jax.sharding import PartitionSpec as P

LMAX = 4
MMAX = 2
NCOEF = 25
KNB = 4
GHOST = 32
NRBF = 16
C = 128
OWN = 128
ROWS = NCOEF * C
WROWS = 115
EDGES = KNB * OWN

EPSILON = 1e-06
SOFTENING = 0.25
STEP_TIME = 0.1
FRICTION = 0.9
RADIAL_SPREAD = 0.5

GROUPS = OWN // GHOST
PER_GROUP = -(-NCOEF // GROUPS)
PACKED = PER_GROUP * C
LAST = (NCOEF - (GROUPS - 1) * PER_GROUP) * C
GROUP_ROWS = (PACKED,) * (GROUPS - 1) + (LAST,)
VMEM_LIMIT = 56 * 1024 * 1024

F32 = jnp.float32
BF16 = jnp.bfloat16


def frame_layout():
    layout = []
    offset = 0
    for degree in range(LMAX + 1):
        row_count = min(2 * degree + 1, 2 * MMAX + 1)
        layout.append((degree, row_count, offset))
        offset = offset + row_count * (2 * degree + 1)
    return layout


LAYOUT = frame_layout()
ORDER_START = (0, 5, 13)
EDGE_ROWS = 19


def edge_row(degree, row):
    if row == 0:
        return degree
    order = (row + 1) // 2
    return ORDER_START[order] + 2 * (degree - order) + (row + 1) % 2


def iota(shape, dim):
    return lax.broadcasted_iota(jnp.int32, shape, dim)


def dot(former, latter):
    return jnp.dot(former, latter, preferred_element_type=F32)


def one_hot(hit):
    return jnp.where(hit, 1.0, 0.0).astype(BF16)


def split_three(values):
    high = values.astype(BF16).astype(F32)
    rest = values - high
    middle = rest.astype(BF16).astype(F32)
    return high, middle, rest - middle


def rim_select(group):
    atom = iota((OWN, 2 * OWN), 0)
    lane = iota((OWN, 2 * OWN), 1)
    low = (lane < OWN) & (lane - GHOST * group == atom) & (atom < GHOST)
    high = (lane >= OWN) & (lane - OWN - GHOST * group == atom - (OWN - GHOST))
    return one_hot(low | (high & (atom >= OWN - GHOST)))


def rim_place(group):
    lane = iota((2 * OWN, OWN), 0)
    atom = iota((2 * OWN, OWN), 1)
    low = (lane < OWN) & (lane - GHOST * group == atom) & (atom < GHOST)
    high = (lane >= OWN) & (lane - OWN - GHOST * group == atom - (OWN - GHOST))
    return one_hot(low | (high & (atom >= OWN - GHOST)))


def pack_rims(read_rows, low_ref, high_ref, extra=None):
    selects = [rim_select(group) for group in range(GROUPS)]
    for block in range(PER_GROUP):
        total = None
        for group in range(GROUPS):
            coef = PER_GROUP * group + block
            if coef < NCOEF:
                part = dot(read_rows(coef * C, C), selects[group])
                total = part if total is None else total + part
        low_ref[pl.ds(block * C, C), :] = total[:, :OWN].astype(BF16)
        high_ref[pl.ds(block * C, C), :] = total[:, OWN:].astype(BF16)
        if extra is not None and block * C == LAST:
            rows = extra.shape[0]
            total = total[:rows] + dot(extra, selects[GROUPS - 1])
            low_ref[pl.ds(block * C, rows), :] = total[:, :OWN].astype(BF16)
            high_ref[pl.ds(block * C, rows), :] = total[:, OWN:].astype(BF16)


def position_parts(pos_ref, parts_ref):
    parts_ref[...] = jnp.zeros_like(parts_ref)
    for at, part in enumerate(split_three(pos_ref[...])):
        parts_ref[pl.ds(8 * at, 3), :] = part
    return parts_ref[...].astype(BF16)


def pack_kernel(feat_ref, pos_ref, low_ref, high_ref, parts_ref):
    parts = position_parts(pos_ref, parts_ref)
    pack_rims(lambda start, size: feat_ref[pl.ds(start, size), :], low_ref, high_ref, parts)


def edge_sources(nb_ref):
    own_at = []
    low_at = []
    high_at = []
    for slot in range(KNB):
        place = jnp.bitwise_and(nb_ref[slot : slot + 1, :], OWN - 1)
        gap = place - iota((1, OWN), 1)
        low = gap > OWN // 2
        high = gap < -(OWN // 2)
        own_at.append(jnp.where(low | high, -1, place))
        low_at.append(jnp.where(low, place - (OWN - GHOST), -1))
        high_at.append(jnp.where(high, place + OWN, -1))
    merge = functools.partial(jnp.concatenate, axis=1)
    return merge(own_at), merge(low_at), merge(high_at)


def own_one_hot(own_at):
    return one_hot(iota((OWN, EDGES), 0) == own_at)


def ghost_one_hot(low_at, high_at, group):
    at = jnp.maximum(low_at, high_at)
    at = jnp.where(at >= 0, at + GHOST * group, -1)
    return one_hot(iota((2 * OWN, EDGES), 0) == at)


def build_gathers(nb_ref, own_ref, ghost_ref):
    own_at, low_at, high_at = edge_sources(nb_ref)
    own_ref[...] = own_one_hot(own_at)
    for group in range(GROUPS):
        ghost_ref[group] = ghost_one_hot(low_at, high_at, group)
    return own_at, low_at, high_at


def corner_mask(block):
    lane = jnp.bitwise_and(iota((C, 2 * OWN), 1), OWN - 1)
    return (lane < OWN - GHOST) | (block * C < LAST)


def read_ghosts(low_ref, high_ref, block):
    low = low_ref[pl.ds(block * C, C), :].astype(F32)
    high = high_ref[pl.ds(block * C, C), :].astype(F32)
    merged = jnp.concatenate([low, high], axis=1)
    if block * C >= LAST:
        merged = jnp.where(corner_mask(block), merged, 0.0)
    return merged


def fold_rows(values):
    return jnp.sum(values.reshape(-1, 8, values.shape[1]), axis=0)


def over_groups(values):
    column = jnp.broadcast_to(jnp.sum(values, axis=0, keepdims=True), values.shape)
    sides = []
    for side in range(2):
        part = column[:, side * OWN : (side + 1) * OWN]
        total = part
        for group in range(1, GROUPS):
            total = total + pltpu.roll(part, GHOST * group, 1)
        sides.append(total)
    return jnp.concatenate(sides, axis=1)[:1]


def normalise(feat_ref, low_ref, high_ref, own_ref, ghost_ref):
    squares = jnp.zeros((8, OWN), F32)
    for coef in range(NCOEF):
        block = feat_ref[pl.ds(coef * C, C), :].astype(F32)
        squares = squares + fold_rows(block * block)
    mean = jnp.sum(squares, axis=0, keepdims=True) * (1.0 / ROWS)
    own_scale = lax.rsqrt(mean + EPSILON)
    for coef in range(NCOEF):
        rows = pl.ds(coef * C, C)
        own_ref[rows, :] = (feat_ref[rows, :].astype(F32) * own_scale).astype(BF16)
    squares = jnp.zeros((8, 2 * OWN), F32)
    for block in range(PER_GROUP):
        values = read_ghosts(low_ref, high_ref, block)
        squares = squares + fold_rows(values * values)
    ghost_scale = lax.rsqrt(over_groups(squares) * (1.0 / ROWS) + EPSILON)
    for block in range(PER_GROUP):
        values = read_ghosts(low_ref, high_ref, block) * ghost_scale
        ghost_ref[pl.ds(block * C, C), :] = values.astype(BF16)
    return own_scale, ghost_scale


def gather(own_ref, ghost_ref, own_hot_ref, ghost_hot_ref, out_ref):
    for group, rows in enumerate(GROUP_ROWS):
        start = group * PACKED
        out_ref[pl.ds(start, rows), :] = dot(
            own_ref[pl.ds(start, rows), :], own_hot_ref[...]
        ) + dot(ghost_ref[pl.ds(0, rows), :], ghost_hot_ref[group])


def twice(values):
    return jnp.concatenate([values, values], axis=0)


def spread_frames(frame_ref, wide_ref):
    for entry in range(WROWS):
        wide_ref[entry] = jnp.broadcast_to(frame_ref[entry : entry + 1, :], (8, EDGES))


def slot_lanes(slot):
    return pl.ds(slot * OWN, OWN)


def to_frame(picked_ref, wide_ref, out_ref):
    @pl.loop(0, C // 16)
    def _(step):
        start = pl.multiple_of(step * 16, 16)
        for slot in range(KNB):
            lanes = slot_lanes(slot)
            for degree, row_count, offset in LAYOUT:
                size = 2 * degree + 1
                parts = [
                    picked_ref[pl.ds((degree * degree + k) * C + start, 16), lanes]
                    for k in range(size)
                ]
                for row in range(row_count):
                    total = None
                    for k in range(size):
                        term = twice(wide_ref[offset + row * size + k, :, lanes]) * parts[k]
                        total = term if total is None else total + term
                    at = edge_row(degree, row) * C
                    out_ref[pl.ds(at + start, 16), lanes] = total.astype(BF16)


def from_frame(frame_rows_ref, wide_ref, out_ref):
    @pl.loop(0, C // 16)
    def _(step):
        start = pl.multiple_of(step * 16, 16)
        for slot in range(KNB):
            lanes = slot_lanes(slot)
            for degree, row_count, offset in LAYOUT:
                size = 2 * degree + 1
                parts = [
                    frame_rows_ref[pl.ds(edge_row(degree, row) * C + start, 16), lanes]
                    for row in range(row_count)
                ]
                for k in range(size):
                    total = None
                    for row in range(row_count):
                        term = twice(wide_ref[offset + row * size + k, :, lanes]) * parts[row]
                        total = term if total is None else total + term
                    at = (degree * degree + k) * C
                    out_ref[pl.ds(at + start, 16), lanes] = total.astype(BF16)


def build_weights(weight_ref, zero_ref, pair_ref):
    turned = [
        jnp.transpose(weight_ref[part].astype(F32)).astype(BF16) for part in range(2 * MMAX + 1)
    ]
    zero_ref[...] = turned[0]
    for order in range(1, MMAX + 1):
        real, imag = turned[2 * order - 1], turned[2 * order]
        pair_ref[order - 1, :C, :C] = real
        pair_ref[order - 1, :C, C:] = -imag
        pair_ref[order - 1, C:, :C] = imag
        pair_ref[order - 1, C:, C:] = real


def build_back_weights(weight_ref, zero_ref, pair_ref):
    zero_ref[...] = weight_ref[0]
    for order in range(1, MMAX + 1):
        real, imag = weight_ref[2 * order - 1], weight_ref[2 * order]
        pair_ref[order - 1, :C, :C] = real
        pair_ref[order - 1, :C, C:] = imag
        pair_ref[order - 1, C:, :C] = -imag
        pair_ref[order - 1, C:, C:] = real


def convolve(rows_ref, zero_ref, pair_ref, out_ref):
    for degree in range(LMAX + 1):
        rows = pl.ds(degree * C, C)
        out_ref[rows, :] = dot(zero_ref[...], rows_ref[rows, :]).astype(out_ref.dtype)
    for order in range(1, MMAX + 1):
        for degree in range(order, LMAX + 1):
            rows = pl.ds((ORDER_START[order] + 2 * (degree - order)) * C, 2 * C)
            out_ref[rows, :] = dot(pair_ref[order - 1], rows_ref[rows, :]).astype(out_ref.dtype)


def radial(distance):
    centers = 0.5 + 5.5 * iota((NRBF, EDGES), 0).astype(F32) / (NRBF - 1)
    offset = (distance - centers) / RADIAL_SPREAD
    return jnp.exp(-(offset * offset)), offset


def edge_gate(radial_ref, basis):
    return lax.dot_general(
        radial_ref[...],
        basis,
        (((0,), (0,)), ((), ())),
        precision=lax.Precision.HIGHEST,
        preferred_element_type=F32,
    )


def distance_slope(radial_ref, gate_slope, distance):
    basis, offset = radial(distance)
    basis_slope = jnp.dot(
        radial_ref[...], gate_slope, precision=lax.Precision.HIGHEST, preferred_element_type=F32
    )
    terms = basis_slope * basis * offset * (-2.0 / RADIAL_SPREAD)
    return jnp.sum(terms, axis=0, keepdims=True)


def message_rows(degree, row_count, offset, start, turned_ref, gate_ref, wide_ref):
    size = 2 * degree + 1
    sums = [None] * size
    for slot in range(KNB):
        lanes = slot_lanes(slot)
        gate = gate_ref[pl.ds(start, 16), lanes]
        for row in range(row_count):
            gated = turned_ref[pl.ds(edge_row(degree, row) * C + start, 16), lanes] * gate
            for k in range(size):
                term = twice(wide_ref[offset + row * size + k, :, lanes]) * gated
                sums[k] = term if sums[k] is None else sums[k] + term
    return sums


def slope_rows(degree, row_count, offset, row, lanes, slopes, wide_ref):
    size = 2 * degree + 1
    total = None
    for k in range(size):
        term = twice(wide_ref[offset + row * size + k, :, lanes]) * slopes[k]
        total = term if total is None else total + term
    return total


def first_kernel(
    feat_ref, low_ref, high_ref, frames_ref, nb_ref, counts_ref, pos_ref, shift_ref,
    weight_ref, radial_ref,
    hidden_ref, turned_ref, frame_out_ref, edge_ref, send_low_ref, send_high_ref,
    parts_ref, own_hot_ref, ghost_hot_ref, own_ref, ghost_ref, picked_ref, wide_ref,
    rows_ref, turned_f32_ref, gate_ref, zero_ref, pair_ref,
):
    column = iota((EDGES, EDGES), 1)
    wanted = jnp.bitwise_and(column, OWN - 1) * KNB + column // OWN
    moved = dot(frames_ref[...], one_hot(iota((EDGES, EDGES), 0) == wanted))
    counts = counts_ref[...]
    live = jnp.concatenate(
        [jnp.where(slot < counts, 1.0, 0.0) for slot in range(KNB)], axis=1
    )
    frame_out_ref[...] = moved * live
    spread_frames(frame_out_ref, wide_ref)
    own_at, low_at, high_at = build_gathers(nb_ref, own_hot_ref, ghost_hot_ref)
    parts = position_parts(pos_ref, parts_ref)
    ghosts = jnp.concatenate(
        [low_ref[pl.ds(LAST, 32), :], high_ref[pl.ds(LAST, 32), :]], axis=1
    )
    found = dot(parts, own_hot_ref[...]) + dot(ghosts, ghost_hot_ref[GROUPS - 1])
    source = (found[0:8] + found[8:16]) + found[16:24]
    shift = jnp.where(low_at >= 0, shift_ref[0], jnp.where(high_at >= 0, shift_ref[1], 0.0))
    first = iota((8, EDGES), 0) == 0
    parts_ref[pl.ds(0, 3), :] = pos_ref[...]
    target = jnp.concatenate([parts_ref[0:8, :]] * KNB, axis=1)
    vector = source + jnp.where(first, shift, 0.0) - target
    distance = jnp.sqrt(jnp.sum(vector * vector, axis=0, keepdims=True) + SOFTENING)
    edge_ref[...] = jnp.where(iota((8, EDGES), 0) == 3, distance, vector)
    gate_ref[...] = edge_gate(radial_ref, radial(distance)[0])
    build_weights(weight_ref, zero_ref, pair_ref)
    normalise(feat_ref, low_ref, high_ref, own_ref, ghost_ref)
    gather(own_ref, ghost_ref, own_hot_ref, ghost_hot_ref, picked_ref)
    to_frame(picked_ref, wide_ref, rows_ref)
    convolve(rows_ref, zero_ref, pair_ref, turned_f32_ref)

    @pl.loop(0, C // 16)
    def _(step):
        start = pl.multiple_of(step * 16, 16)
        for degree, row_count, offset in LAYOUT:
            sums = message_rows(
                degree, row_count, offset, start, turned_f32_ref, gate_ref, wide_ref
            )
            for k, total in enumerate(sums):
                rows = pl.ds((degree * degree + k) * C + start, 16)
                hidden = feat_ref[rows, :].astype(F32) + total * KNB ** (-0.5)
                hidden_ref[rows, :] = hidden.astype(BF16)
        for row in range(EDGE_ROWS):
            rows = pl.ds(row * C + start, 16)
            turned_ref[rows, :] = turned_f32_ref[rows, :].astype(BF16)

    pack_rims(lambda start, size: hidden_ref[pl.ds(start, size), :], send_low_ref, send_high_ref)


def second_kernel(
    feat_ref, low_ref, high_ref, frame_ref, nb_ref, edge_ref, weight_ref, radial_ref,
    readout_ref,
    slope_ref, distance_slope_ref, send_low_ref, send_high_ref,
    own_hot_ref, ghost_hot_ref, own_ref, ghost_ref, picked_ref, wide_ref, rows_ref,
    turned_ref, gate_ref, zero_ref, pair_ref, upper_ref, gate_slope_ref, turned_slope_ref,
    readout_wide_ref, edge_slope_ref, ghost_slope_ref,
):
    spread_frames(frame_ref, wide_ref)
    build_gathers(nb_ref, own_hot_ref, ghost_hot_ref)
    distance = edge_ref[3:4, :]
    gate_ref[...] = edge_gate(radial_ref, radial(distance)[0])
    build_weights(weight_ref, zero_ref, pair_ref)
    own_scale, ghost_scale = normalise(feat_ref, low_ref, high_ref, own_ref, ghost_ref)
    gather(own_ref, ghost_ref, own_hot_ref, ghost_hot_ref, picked_ref)
    to_frame(picked_ref, wide_ref, rows_ref)
    convolve(rows_ref, zero_ref, pair_ref, turned_ref)
    for degree in range(LMAX + 1):
        row = jnp.broadcast_to(readout_ref[degree : degree + 1, :], (C, C))
        readout_wide_ref[degree] = jnp.transpose(row) * (1.0 / (2 * degree + 1))

    @pl.loop(0, C // 16)
    def _(step):
        start = pl.multiple_of(step * 16, 16)
        channels = pl.ds(start, 16)
        gate_slopes = [None] * KNB
        for degree, row_count, offset in LAYOUT:
            sums = message_rows(degree, row_count, offset, start, turned_ref, gate_ref, wide_ref)
            weight = readout_wide_ref[degree, channels, :]
            slopes = []
            for k, total in enumerate(sums):
                rows = pl.ds((degree * degree + k) * C + start, 16)
                upper = feat_ref[rows, :].astype(F32) + total * KNB ** (-0.5)
                slope = upper * weight
                upper_ref[rows, :] = slope * 2.0
                slopes.append(slope * (2.0 * KNB ** (-0.5)))
            for slot in range(KNB):
                lanes = slot_lanes(slot)
                gate = gate_ref[channels, lanes]
                for row in range(row_count):
                    slope = slope_rows(
                        degree, row_count, offset, row, lanes, slopes, wide_ref
                    )
                    rows = pl.ds(edge_row(degree, row) * C + start, 16)
                    term = turned_ref[rows, lanes] * slope
                    before = gate_slopes[slot]
                    gate_slopes[slot] = term if before is None else before + term
                    turned_slope_ref[rows, lanes] = (slope * gate).astype(BF16)
        for slot in range(KNB):
            gate_slope_ref[channels, slot_lanes(slot)] = gate_slopes[slot]

    distance_slope_ref[...] = jnp.broadcast_to(
        distance_slope(radial_ref, gate_slope_ref[...], distance), (8, EDGES)
    )
    build_back_weights(weight_ref, zero_ref, pair_ref)
    convolve(turned_slope_ref, zero_ref, pair_ref, turned_ref)
    from_frame(turned_ref, wide_ref, edge_slope_ref)
    spread_own = jnp.transpose(own_hot_ref[...].astype(F32)).astype(BF16)
    for group, rows in enumerate(GROUP_ROWS):
        block = pl.ds(group * PACKED, rows)
        slope_ref[block, :] = dot(edge_slope_ref[block, :], spread_own)
    for group, rows in enumerate(GROUP_ROWS):
        spread_ghost = jnp.transpose(ghost_hot_ref[group].astype(F32)).astype(BF16)
        part = dot(edge_slope_ref[pl.ds(group * PACKED, rows), :], spread_ghost)
        if group == 0:
            ghost_slope_ref[...] = part
        else:
            ghost_slope_ref[pl.ds(0, rows), :] += part
    along = jnp.zeros((8, OWN), F32)
    for coef in range(NCOEF):
        rows = pl.ds(coef * C, C)
        along = along + fold_rows(slope_ref[rows, :] * feat_ref[rows, :].astype(F32))
    along = jnp.sum(along, axis=0, keepdims=True) * (1.0 / ROWS)
    along = along * own_scale * own_scale * own_scale
    for coef in range(NCOEF):
        rows = pl.ds(coef * C, C)
        slope_ref[rows, :] = (
            upper_ref[rows, :]
            + slope_ref[rows, :] * own_scale
            - feat_ref[rows, :].astype(F32) * along
        )
    along = jnp.zeros((8, 2 * OWN), F32)
    for block in range(PER_GROUP):
        values = read_ghosts(low_ref, high_ref, block)
        along = along + fold_rows(ghost_slope_ref[pl.ds(block * C, C), :] * values)
    along = over_groups(along) * (1.0 / ROWS)
    along = along * ghost_scale * ghost_scale * ghost_scale
    for block in range(PER_GROUP):
        rows = pl.ds(block * C, C)
        values = read_ghosts(low_ref, high_ref, block)
        back = ghost_slope_ref[rows, :] * ghost_scale - values * along
        send_low_ref[rows, :] = back[:, :OWN].astype(BF16)
        send_high_ref[rows, :] = back[:, OWN:].astype(BF16)


def third_kernel(
    slope_ref, low_ref, high_ref, frame_ref, nb_ref, edge_ref, radial_ref, turned_ref,
    second_slope_ref,
    force_ref, ghost_low_ref, ghost_high_ref, virial_ref,
    wide_ref, gate_slope_ref, hidden_slope_ref,
):
    spread_frames(frame_ref, wide_ref)
    for group, rows in enumerate(GROUP_ROWS):
        block = pl.ds(group * PACKED, rows)
        back = jnp.concatenate([low_ref[pl.ds(0, rows), :], high_ref[pl.ds(0, rows), :]], axis=1)
        total = slope_ref[block, :] + dot(back, rim_place(group))
        hidden_slope_ref[block, :] = total * KNB ** (-0.5)

    @pl.loop(0, C // 16)
    def _(step):
        start = pl.multiple_of(step * 16, 16)
        gate_slopes = [None] * KNB
        for degree, row_count, offset in LAYOUT:
            slopes = [
                hidden_slope_ref[pl.ds((degree * degree + k) * C + start, 16), :]
                for k in range(2 * degree + 1)
            ]
            for slot in range(KNB):
                lanes = slot_lanes(slot)
                for row in range(row_count):
                    slope = slope_rows(
                        degree, row_count, offset, row, lanes, slopes, wide_ref
                    )
                    rows = pl.ds(edge_row(degree, row) * C + start, 16)
                    term = turned_ref[rows, lanes].astype(F32) * slope
                    before = gate_slopes[slot]
                    gate_slopes[slot] = term if before is None else before + term
        for slot in range(KNB):
            gate_slope_ref[pl.ds(start, 16), slot_lanes(slot)] = gate_slopes[slot]

    distance = edge_ref[3:4, :]
    slope = distance_slope(radial_ref, gate_slope_ref[...], distance) + second_slope_ref[0:1, :]
    vector = jnp.where(iota((8, EDGES), 0) < 3, edge_ref[...], 0.0)
    pull = vector * (slope / distance)
    virial = -jnp.sum(jnp.sum(pull * vector, axis=0, keepdims=True), axis=1, keepdims=True)
    virial_ref[...] = jnp.broadcast_to(virial, (8, OWN))
    high, middle, low = split_three(pull)
    parts = jnp.concatenate([high, middle, low, jnp.zeros((8, EDGES), F32)], axis=0).astype(BF16)
    own_at, low_at, high_at = edge_sources(nb_ref)
    spread_own = jnp.transpose(own_one_hot(own_at).astype(F32)).astype(BF16)
    spread_ghost = jnp.transpose(ghost_one_hot(low_at, high_at, 0).astype(F32)).astype(BF16)
    landed = dot(parts, spread_own)
    landed = landed[0:8] + landed[8:16] + landed[16:24]
    for slot in range(KNB):
        landed = landed - pull[:, slot * OWN : (slot + 1) * OWN]
    force_ref[...] = -landed
    landed = dot(parts, spread_ghost)
    landed = landed[0:8] + landed[8:16] + landed[16:24]
    ghost_low_ref[...] = -landed[:, :OWN]
    ghost_high_ref[...] = -landed[:, OWN:]


def kick_kernel(
    force_ref, low_ref, high_ref, virial_ref, velocities_ref, masses_ref,
    kicked_ref, strain_ref,
):
    lane = iota((8, OWN), 1)
    force = force_ref[...] + jnp.where(lane < GHOST, low_ref[...], 0.0)
    high = pltpu.roll(high_ref[...], OWN - GHOST, 1)
    force = force + jnp.where(lane >= OWN - GHOST, high, 0.0)
    masses = masses_ref[...]
    kicked = velocities_ref[...] + STEP_TIME * force[0:3] / masses
    kicked_ref[...] = kicked
    total = jnp.sum(masses * jnp.sum(kicked * kicked, axis=0, keepdims=True))
    strain_ref[...] = virial_ref[...] + total


def finish_kernel(
    strain_ref, kicked_ref, masses_ref, noise_ref, positions_ref, box_ref, control_ref,
    fractional_ref, velocities_ref, new_box_ref,
):
    row = iota((3, OWN), 0)
    box = jnp.where(row == 0, box_ref[0], jnp.where(row == 1, box_ref[1], box_ref[2]))
    volume = box_ref[0] * box_ref[1] * box_ref[2]
    pressure = strain_ref[0:1, :] / (3.0 * volume)
    rescale = jnp.exp(control_ref[1] * (pressure - control_ref[2]) / 3.0)
    kick = jnp.sqrt((1.0 - FRICTION * FRICTION) * control_ref[0] / masses_ref[...])
    thermal = FRICTION * kicked_ref[...] + kick * noise_ref[...]
    fractional_ref[...] = (positions_ref[...] + STEP_TIME * thermal) / box
    velocities_ref[...] = thermal / rescale
    new_box_ref[...] = box * rescale


def call(kernel, outs, scratch, args, flops=0, scalars=(), moved=4 << 20):
    specs = [
        pl.BlockSpec(memory_space=pltpu.SMEM if at in scalars else pltpu.VMEM)
        for at in range(len(args))
    ]
    return pl.pallas_call(
        kernel,
        out_shape=[jax.ShapeDtypeStruct(shape, kind) for shape, kind in outs],
        in_specs=specs,
        out_specs=[pl.BlockSpec(memory_space=pltpu.VMEM) for _ in outs],
        scratch_shapes=[pltpu.VMEM(shape, kind) for shape, kind in scratch],
        compiler_params=pltpu.CompilerParams(vmem_limit_bytes=VMEM_LIMIT),
        cost_estimate=pl.CostEstimate(flops=flops, bytes_accessed=moved, transcendentals=0),
    )(*args)


def shards(
    node_feat,
    frames,
    neighbours,
    counts,
    positions,
    velocities,
    masses,
    thermal_noise,
    box_lengths,
    control,
    conv_weight,
    radial_weight,
    readout,
):
    assert positions.shape[1] == OWN
    count = lax.axis_size("gx")
    place = lax.axis_index("gx")
    forward = [(i, (i + 1) % count) for i in range(count)]
    backward = [(target, source) for source, target in forward]

    def exchange(to_low, to_high):
        from_low = lax.ppermute(to_high, "gx", forward)
        from_high = lax.ppermute(to_low, "gx", backward)
        return from_low, from_high

    packed = ((PACKED, OWN), BF16)
    to_low, to_high = call(
        pack_kernel, [packed, packed], [((32, OWN), F32)], (node_feat, positions)
    )
    from_low, from_high = exchange(to_low, to_high)
    length = box_lengths[0]
    shift = jnp.stack(
        [
            jnp.where(place == 0, -length, 0.0),
            jnp.where(place == count - 1, length, 0.0),
        ]
    )
    gathers = [((OWN, EDGES), BF16), ((GROUPS, 2 * OWN, EDGES), BF16)]
    work = [
        ((ROWS, OWN), BF16),
        ((PACKED, 2 * OWN), BF16),
        ((ROWS, EDGES), F32),
        ((WROWS, 8, EDGES), F32),
        ((EDGE_ROWS * C, EDGES), BF16),
        ((EDGE_ROWS * C, EDGES), F32),
        ((C, EDGES), F32),
        ((C, C), BF16),
        ((MMAX, 2 * C, 2 * C), BF16),
    ]
    hidden, turned, frame, edge, to_low, to_high = call(
        first_kernel,
        [
            ((ROWS, OWN), BF16),
            ((EDGE_ROWS * C, EDGES), BF16),
            ((WROWS, EDGES), F32),
            ((8, EDGES), F32),
            packed,
            packed,
        ],
        [((32, OWN), F32)] + gathers + work,
        (
            node_feat, from_low, from_high, frames, neighbours, counts[None, :], positions,
            shift, conv_weight[0], radial_weight[0],
        ),
        scalars=(7,),
    )
    from_low, from_high = exchange(to_low, to_high)
    slope, second_slope, to_low, to_high = call(
        second_kernel,
        [((ROWS, OWN), F32), ((8, EDGES), F32), packed, packed],
        gathers
        + work
        + [
            ((ROWS, OWN), F32),
            ((C, EDGES), F32),
            ((EDGE_ROWS * C, EDGES), BF16),
            ((LMAX + 1, C, C), F32),
            ((ROWS, EDGES), BF16),
            ((PACKED, 2 * OWN), F32),
        ],
        (
            hidden, from_low, from_high, frame, neighbours, edge, conv_weight[1],
            radial_weight[1], readout,
        ),
    )
    from_low, from_high = exchange(to_low, to_high)
    small = ((8, OWN), F32)
    force, to_low, to_high, virial = call(
        third_kernel,
        [small] * 4,
        [((WROWS, 8, EDGES), F32), ((C, EDGES), F32), ((ROWS, OWN), F32)],
        (
            slope, from_low, from_high, frame, neighbours, edge, radial_weight[0], turned,
            second_slope,
        ),
    )
    from_low, from_high = exchange(to_low, to_high)
    kicked, strain = call(
        kick_kernel,
        [((3, OWN), F32), small],
        [],
        (force, from_low, from_high, virial, velocities, masses[None, :]),
    )
    if count & (count - 1) == 0:
        step = 1
        while step < count:
            strain = strain + lax.ppermute(strain, "gx", [(i, i ^ step) for i in range(count)])
            step = 2 * step
    else:
        strain = lax.psum(strain, "gx")
    fractional, new_velocities, new_box = call(
        finish_kernel,
        [((3, OWN), F32)] * 3,
        [],
        (strain, kicked, masses[None, :], thermal_noise, positions, box_lengths, control),
        scalars=(5, 6),
    )
    return fractional, new_velocities, new_box[:, 0]


def solution(mesh):
    return jax.shard_map(
        shards,
        mesh=mesh,
        in_specs=(
            P(None, ("groups", "gx")),
            P(None, ("groups", "gx")),
            P(None, ("groups", "gx")),
            P(("groups", "gx")),
            P(None, ("groups", "gx")),
            P(None, ("groups", "gx")),
            P(("groups", "gx")),
            P(None, ("groups", "gx")),
            P("groups"),
            P("groups"),
            P(),
            P(),
            P(),
        ),
        out_specs=(P(None, ("groups", "gx")), P(None, ("groups", "gx")), P("groups")),
        check_vma=False,
    )
```

```python
import functools

import jax
import jax.numpy as jnp
from jax import lax
from jax.experimental import pallas as pl
from jax.experimental.pallas import tpu as pltpu
from jax.sharding import PartitionSpec as P

LMAX = 4
MMAX = 2
NCOEF = 25
KNB = 4
GHOST = 32
NRBF = 16
C = 128
OWN = 128
ROWS = NCOEF * C
WROWS = 115
EDGES = KNB * OWN

EPSILON = 1e-06
SOFTENING = 0.25
STEP_TIME = 0.1
FRICTION = 0.9
RADIAL_SPREAD = 0.5

GROUPS = OWN // GHOST
PER_GROUP = -(-NCOEF // GROUPS)
PACKED = PER_GROUP * C
LAST = (NCOEF - (GROUPS - 1) * PER_GROUP) * C
GROUP_ROWS = (PACKED,) * (GROUPS - 1) + (LAST,)
GRANTS = (28, 36, 14)

F32 = jnp.float32
BF16 = jnp.bfloat16


def frame_layout():
    layout = []
    offset = 0
    for degree in range(LMAX + 1):
        row_count = min(2 * degree + 1, 2 * MMAX + 1)
        layout.append((degree, row_count, offset))
        offset = offset + row_count * (2 * degree + 1)
    return layout


LAYOUT = frame_layout()
ORDER_START = (0, 5, 13)
EDGE_ROWS = 19


def edge_row(degree, row):
    if row == 0:
        return degree
    order = (row + 1) // 2
    return ORDER_START[order] + 2 * (degree - order) + (row + 1) % 2


def iota(shape, dim):
    return lax.broadcasted_iota(jnp.int32, shape, dim)


def dot(former, latter):
    return jnp.dot(former, latter, preferred_element_type=F32)


def one_hot(hit):
    return jnp.where(hit, 1.0, 0.0).astype(BF16)


def split_three(values):
    high = values.astype(BF16).astype(F32)
    rest = values - high
    middle = rest.astype(BF16).astype(F32)
    return high, middle, rest - middle


def rim_select(group):
    atom = iota((OWN, 2 * OWN), 0)
    lane = iota((OWN, 2 * OWN), 1)
    low = (lane < OWN) & (lane - GHOST * group == atom) & (atom < GHOST)
    high = (lane >= OWN) & (lane - OWN - GHOST * group == atom - (OWN - GHOST))
    return one_hot(low | (high & (atom >= OWN - GHOST)))


def rim_place(group):
    lane = iota((2 * OWN, OWN), 0)
    atom = iota((2 * OWN, OWN), 1)
    low = (lane < OWN) & (lane - GHOST * group == atom) & (atom < GHOST)
    high = (lane >= OWN) & (lane - OWN - GHOST * group == atom - (OWN - GHOST))
    return one_hot(low | (high & (atom >= OWN - GHOST)))


def pack_rims(read_rows, low_ref, high_ref, extra=None):
    selects = [rim_select(group) for group in range(GROUPS)]
    for block in range(PER_GROUP):
        total = None
        for group in range(GROUPS):
            coef = PER_GROUP * group + block
            if coef < NCOEF:
                part = dot(read_rows(coef * C, C), selects[group])
                total = part if total is None else total + part
        low_ref[pl.ds(block * C, C), :] = total[:, :OWN].astype(BF16)
        high_ref[pl.ds(block * C, C), :] = total[:, OWN:].astype(BF16)
        if extra is not None and block * C == LAST:
            rows = extra.shape[0]
            total = total[:rows] + dot(extra, selects[GROUPS - 1])
            low_ref[pl.ds(block * C, rows), :] = total[:, :OWN].astype(BF16)
            high_ref[pl.ds(block * C, rows), :] = total[:, OWN:].astype(BF16)


def position_parts(pos_ref, parts_ref):
    parts_ref[...] = jnp.zeros_like(parts_ref)
    for at, part in enumerate(split_three(pos_ref[...])):
        parts_ref[pl.ds(8 * at, 3), :] = part
    return parts_ref[...].astype(BF16)


def pack_kernel(feat_ref, pos_ref, low_ref, high_ref, parts_ref):
    parts = position_parts(pos_ref, parts_ref)
    pack_rims(lambda start, size: feat_ref[pl.ds(start, size), :], low_ref, high_ref, parts)


def edge_sources(nb_ref):
    own_at = []
    low_at = []
    high_at = []
    for slot in range(KNB):
        place = jnp.bitwise_and(nb_ref[slot : slot + 1, :], OWN - 1)
        gap = place - iota((1, OWN), 1)
        low = gap > OWN // 2
        high = gap < -(OWN // 2)
        own_at.append(jnp.where(low | high, -1, place))
        low_at.append(jnp.where(low, place - (OWN - GHOST), -1))
        high_at.append(jnp.where(high, place + OWN, -1))
    merge = functools.partial(jnp.concatenate, axis=1)
    return merge(own_at), merge(low_at), merge(high_at)


def own_one_hot(own_at):
    return one_hot(iota((OWN, EDGES), 0) == own_at)


def ghost_one_hot(low_at, high_at, group):
    at = jnp.maximum(low_at, high_at)
    at = jnp.where(at >= 0, at + GHOST * group, -1)
    return one_hot(iota((2 * OWN, EDGES), 0) == at)


def build_gathers(nb_ref, own_ref, ghost_ref):
    own_at, low_at, high_at = edge_sources(nb_ref)
    own_ref[...] = own_one_hot(own_at)
    for group in range(GROUPS):
        ghost_ref[group] = ghost_one_hot(low_at, high_at, group)
    return own_at, low_at, high_at


def corner_mask(block):
    lane = jnp.bitwise_and(iota((C, 2 * OWN), 1), OWN - 1)
    return (lane < OWN - GHOST) | (block * C < LAST)


def read_ghosts(low_ref, high_ref, block):
    low = low_ref[pl.ds(block * C, C), :].astype(F32)
    high = high_ref[pl.ds(block * C, C), :].astype(F32)
    merged = jnp.concatenate([low, high], axis=1)
    if block * C >= LAST:
        merged = jnp.where(corner_mask(block), merged, 0.0)
    return merged


def fold_rows(values):
    return jnp.sum(values.reshape(-1, 8, values.shape[1]), axis=0)


def over_groups(values):
    column = jnp.broadcast_to(jnp.sum(values, axis=0, keepdims=True), values.shape)
    sides = []
    for side in range(2):
        part = column[:, side * OWN : (side + 1) * OWN]
        total = part
        for group in range(1, GROUPS):
            total = total + pltpu.roll(part, GHOST * group, 1)
        sides.append(total)
    return jnp.concatenate(sides, axis=1)[:1]


def normalise(feat_ref, low_ref, high_ref, own_ref, ghost_ref):
    squares = jnp.zeros((8, OWN), F32)
    for coef in range(NCOEF):
        block = feat_ref[pl.ds(coef * C, C), :].astype(F32)
        squares = squares + fold_rows(block * block)
    mean = jnp.sum(squares, axis=0, keepdims=True) * (1.0 / ROWS)
    own_scale = lax.rsqrt(mean + EPSILON)
    for coef in range(NCOEF):
        rows = pl.ds(coef * C, C)
        own_ref[rows, :] = (feat_ref[rows, :].astype(F32) * own_scale).astype(BF16)
    squares = jnp.zeros((8, 2 * OWN), F32)
    for block in range(PER_GROUP):
        values = read_ghosts(low_ref, high_ref, block)
        squares = squares + fold_rows(values * values)
    ghost_scale = lax.rsqrt(over_groups(squares) * (1.0 / ROWS) + EPSILON)
    for block in range(PER_GROUP):
        values = read_ghosts(low_ref, high_ref, block) * ghost_scale
        ghost_ref[pl.ds(block * C, C), :] = values.astype(BF16)
    return own_scale, ghost_scale


def gather(own_ref, ghost_ref, own_hot_ref, ghost_hot_ref, out_ref):
    for group, rows in enumerate(GROUP_ROWS):
        start = group * PACKED
        out_ref[pl.ds(start, rows), :] = dot(
            own_ref[pl.ds(start, rows), :], own_hot_ref[...]
        ) + dot(ghost_ref[pl.ds(0, rows), :], ghost_hot_ref[group])


def twice(values):
    return jnp.concatenate([values, values], axis=0)


def spread_frames(frame_ref, wide_ref):
    for entry in range(WROWS):
        wide_ref[entry] = jnp.broadcast_to(frame_ref[entry : entry + 1, :], (8, EDGES))


def slot_lanes(slot):
    return pl.ds(slot * OWN, OWN)


def to_frame(picked_ref, wide_ref, out_ref):
    @pl.loop(0, C // 16)
    def _(step):
        start = pl.multiple_of(step * 16, 16)
        for slot in range(KNB):
            lanes = slot_lanes(slot)
            for degree, row_count, offset in LAYOUT:
                size = 2 * degree + 1
                parts = [
                    picked_ref[pl.ds((degree * degree + k) * C + start, 16), lanes]
                    for k in range(size)
                ]
                for row in range(row_count):
                    total = None
                    for k in range(size):
                        term = twice(wide_ref[offset + row * size + k, :, lanes]) * parts[k]
                        total = term if total is None else total + term
                    at = edge_row(degree, row) * C
                    out_ref[pl.ds(at + start, 16), lanes] = total.astype(BF16)


def from_frame(frame_rows_ref, wide_ref, out_ref):
    @pl.loop(0, C // 16)
    def _(step):
        start = pl.multiple_of(step * 16, 16)
        for slot in range(KNB):
            lanes = slot_lanes(slot)
            for degree, row_count, offset in LAYOUT:
                size = 2 * degree + 1
                parts = [
                    frame_rows_ref[pl.ds(edge_row(degree, row) * C + start, 16), lanes]
                    for row in range(row_count)
                ]
                for k in range(size):
                    total = None
                    for row in range(row_count):
                        term = twice(wide_ref[offset + row * size + k, :, lanes]) * parts[row]
                        total = term if total is None else total + term
                    at = (degree * degree + k) * C
                    out_ref[pl.ds(at + start, 16), lanes] = total.astype(BF16)


def build_weights(weight_ref, zero_ref, pair_ref):
    turned = [
        jnp.transpose(weight_ref[part].astype(F32)).astype(BF16) for part in range(2 * MMAX + 1)
    ]
    zero_ref[...] = turned[0]
    for order in range(1, MMAX + 1):
        real, imag = turned[2 * order - 1], turned[2 * order]
        pair_ref[order - 1, :C, :C] = real
        pair_ref[order - 1, :C, C:] = -imag
        pair_ref[order - 1, C:, :C] = imag
        pair_ref[order - 1, C:, C:] = real


def build_back_weights(weight_ref, zero_ref, pair_ref):
    zero_ref[...] = weight_ref[0]
    for order in range(1, MMAX + 1):
        real, imag = weight_ref[2 * order - 1], weight_ref[2 * order]
        pair_ref[order - 1, :C, :C] = real
        pair_ref[order - 1, :C, C:] = imag
        pair_ref[order - 1, C:, :C] = -imag
        pair_ref[order - 1, C:, C:] = real


def convolve(rows_ref, zero_ref, pair_ref, out_ref):
    for degree in range(LMAX + 1):
        rows = pl.ds(degree * C, C)
        out_ref[rows, :] = dot(zero_ref[...], rows_ref[rows, :]).astype(out_ref.dtype)
    for order in range(1, MMAX + 1):
        for degree in range(order, LMAX + 1):
            rows = pl.ds((ORDER_START[order] + 2 * (degree - order)) * C, 2 * C)
            out_ref[rows, :] = dot(pair_ref[order - 1], rows_ref[rows, :]).astype(out_ref.dtype)


def radial(distance):
    centers = 0.5 + 5.5 * iota((NRBF, EDGES), 0).astype(F32) / (NRBF - 1)
    offset = (distance - centers) / RADIAL_SPREAD
    return jnp.exp(-(offset * offset)), offset


def edge_gate(radial_ref, basis):
    return lax.dot_general(
        radial_ref[...],
        basis,
        (((0,), (0,)), ((), ())),
        precision=lax.Precision.HIGHEST,
        preferred_element_type=F32,
    )


def distance_slope(radial_ref, gate_slope, distance):
    basis, offset = radial(distance)
    basis_slope = jnp.dot(
        radial_ref[...], gate_slope, precision=lax.Precision.HIGHEST, preferred_element_type=F32
    )
    terms = basis_slope * basis * offset * (-2.0 / RADIAL_SPREAD)
    return jnp.sum(terms, axis=0, keepdims=True)


def message_rows(degree, row_count, offset, start, turned_ref, gate_ref, wide_ref):
    size = 2 * degree + 1
    sums = [None] * size
    for slot in range(KNB):
        lanes = slot_lanes(slot)
        gate = gate_ref[pl.ds(start, 16), lanes]
        for row in range(row_count):
            gated = turned_ref[pl.ds(edge_row(degree, row) * C + start, 16), lanes] * gate
            for k in range(size):
                term = twice(wide_ref[offset + row * size + k, :, lanes]) * gated
                sums[k] = term if sums[k] is None else sums[k] + term
    return sums


def slope_rows(degree, row_count, offset, row, lanes, slopes, wide_ref):
    size = 2 * degree + 1
    total = None
    for k in range(size):
        term = twice(wide_ref[offset + row * size + k, :, lanes]) * slopes[k]
        total = term if total is None else total + term
    return total


def first_kernel(
    feat_ref, low_ref, high_ref, frames_ref, nb_ref, counts_ref, pos_ref, box_ref,
    weight_ref, radial_ref,
    hidden_ref, turned_ref, frame_out_ref, edge_ref, send_low_ref, send_high_ref,
    parts_ref, own_hot_ref, ghost_hot_ref, own_ref, ghost_ref, picked_ref, wide_ref,
    rows_ref, turned_f32_ref, gate_ref, zero_ref, pair_ref,
):
    column = iota((EDGES, EDGES), 1)
    wanted = jnp.bitwise_and(column, OWN - 1) * KNB + column // OWN
    moved = dot(frames_ref[...], one_hot(iota((EDGES, EDGES), 0) == wanted))
    counts = counts_ref[...]
    live = jnp.concatenate(
        [jnp.where(slot < counts, 1.0, 0.0) for slot in range(KNB)], axis=1
    )
    frame_out_ref[...] = moved * live
    spread_frames(frame_out_ref, wide_ref)
    own_at, low_at, high_at = build_gathers(nb_ref, own_hot_ref, ghost_hot_ref)
    parts = position_parts(pos_ref, parts_ref)
    ghosts = jnp.concatenate(
        [low_ref[pl.ds(LAST, 32), :], high_ref[pl.ds(LAST, 32), :]], axis=1
    )
    found = dot(parts, own_hot_ref[...]) + dot(ghosts, ghost_hot_ref[GROUPS - 1])
    source = (found[0:8] + found[8:16]) + found[16:24]
    place = lax.axis_index("gx")
    low_shift = jnp.where(place == 0, -box_ref[0], 0.0)
    high_shift = jnp.where(place == lax.axis_size("gx") - 1, box_ref[0], 0.0)
    shift = jnp.where(low_at >= 0, low_shift, jnp.where(high_at >= 0, high_shift, 0.0))
    first = iota((8, EDGES), 0) == 0
    parts_ref[pl.ds(0, 3), :] = pos_ref[...]
    target = jnp.concatenate([parts_ref[0:8, :]] * KNB, axis=1)
    vector = source + jnp.where(first, shift, 0.0) - target
    distance = jnp.sqrt(jnp.sum(vector * vector, axis=0, keepdims=True) + SOFTENING)
    edge_ref[...] = jnp.where(iota((8, EDGES), 0) == 3, distance, vector)
    gate_ref[...] = edge_gate(radial_ref, radial(distance)[0])
    build_weights(weight_ref, zero_ref, pair_ref)
    normalise(feat_ref, low_ref, high_ref, own_ref, ghost_ref)
    gather(own_ref, ghost_ref, own_hot_ref, ghost_hot_ref, picked_ref)
    to_frame(picked_ref, wide_ref, rows_ref)
    convolve(rows_ref, zero_ref, pair_ref, turned_f32_ref)

    @pl.loop(0, C // 16)
    def _(step):
        start = pl.multiple_of(step * 16, 16)
        for degree, row_count, offset in LAYOUT:
            sums = message_rows(
                degree, row_count, offset, start, turned_f32_ref, gate_ref, wide_ref
            )
            for k, total in enumerate(sums):
                rows = pl.ds((degree * degree + k) * C + start, 16)
                hidden = feat_ref[rows, :].astype(F32) + total * KNB ** (-0.5)
                hidden_ref[rows, :] = hidden.astype(BF16)
        for row in range(EDGE_ROWS):
            rows = pl.ds(row * C + start, 16)
            turned_ref[rows, :] = turned_f32_ref[rows, :].astype(BF16)

    pack_rims(lambda start, size: hidden_ref[pl.ds(start, size), :], send_low_ref, send_high_ref)


def second_kernel(
    feat_ref, low_ref, high_ref, frame_ref, nb_ref, edge_ref, weight_ref, radial_ref,
    readout_ref,
    slope_ref, distance_slope_ref, send_low_ref, send_high_ref,
    own_hot_ref, ghost_hot_ref, own_ref, ghost_ref, picked_ref, wide_ref, rows_ref,
    turned_ref, gate_ref, zero_ref, pair_ref, upper_ref, gate_slope_ref, turned_slope_ref,
    readout_wide_ref, edge_slope_ref, ghost_slope_ref,
):
    spread_frames(frame_ref, wide_ref)
    build_gathers(nb_ref, own_hot_ref, ghost_hot_ref)
    distance = edge_ref[3:4, :]
    gate_ref[...] = edge_gate(radial_ref, radial(distance)[0])
    build_weights(weight_ref, zero_ref, pair_ref)
    own_scale, ghost_scale = normalise(feat_ref, low_ref, high_ref, own_ref, ghost_ref)
    gather(own_ref, ghost_ref, own_hot_ref, ghost_hot_ref, picked_ref)
    to_frame(picked_ref, wide_ref, rows_ref)
    convolve(rows_ref, zero_ref, pair_ref, turned_ref)
    for degree in range(LMAX + 1):
        row = jnp.broadcast_to(readout_ref[degree : degree + 1, :], (C, C))
        readout_wide_ref[degree] = jnp.transpose(row) * (1.0 / (2 * degree + 1))

    @pl.loop(0, C // 16)
    def _(step):
        start = pl.multiple_of(step * 16, 16)
        channels = pl.ds(start, 16)
        gate_slopes = [None] * KNB
        for degree, row_count, offset in LAYOUT:
            sums = message_rows(degree, row_count, offset, start, turned_ref, gate_ref, wide_ref)
            weight = readout_wide_ref[degree, channels, :]
            slopes = []
            for k, total in enumerate(sums):
                rows = pl.ds((degree * degree + k) * C + start, 16)
                upper = feat_ref[rows, :].astype(F32) + total * KNB ** (-0.5)
                slope = upper * weight
                upper_ref[rows, :] = slope * 2.0
                slopes.append(slope * (2.0 * KNB ** (-0.5)))
            for slot in range(KNB):
                lanes = slot_lanes(slot)
                gate = gate_ref[channels, lanes]
                for row in range(row_count):
                    slope = slope_rows(
                        degree, row_count, offset, row, lanes, slopes, wide_ref
                    )
                    rows = pl.ds(edge_row(degree, row) * C + start, 16)
                    term = turned_ref[rows, lanes] * slope
                    before = gate_slopes[slot]
                    gate_slopes[slot] = term if before is None else before + term
                    turned_slope_ref[rows, lanes] = (slope * gate).astype(BF16)
        for slot in range(KNB):
            gate_slope_ref[channels, slot_lanes(slot)] = gate_slopes[slot]

    distance_slope_ref[...] = jnp.broadcast_to(
        distance_slope(radial_ref, gate_slope_ref[...], distance), (8, EDGES)
    )
    build_back_weights(weight_ref, zero_ref, pair_ref)
    convolve(turned_slope_ref, zero_ref, pair_ref, turned_ref)
    from_frame(turned_ref, wide_ref, edge_slope_ref)
    spread_own = jnp.transpose(own_hot_ref[...].astype(F32)).astype(BF16)
    for group, rows in enumerate(GROUP_ROWS):
        block = pl.ds(group * PACKED, rows)
        slope_ref[block, :] = dot(edge_slope_ref[block, :], spread_own)
    for group, rows in enumerate(GROUP_ROWS):
        spread_ghost = jnp.transpose(ghost_hot_ref[group].astype(F32)).astype(BF16)
        part = dot(edge_slope_ref[pl.ds(group * PACKED, rows), :], spread_ghost)
        if group == 0:
            ghost_slope_ref[...] = part
        else:
            ghost_slope_ref[pl.ds(0, rows), :] += part
    along = jnp.zeros((8, OWN), F32)
    for coef in range(NCOEF):
        rows = pl.ds(coef * C, C)
        along = along + fold_rows(slope_ref[rows, :] * feat_ref[rows, :].astype(F32))
    along = jnp.sum(along, axis=0, keepdims=True) * (1.0 / ROWS)
    along = along * own_scale * own_scale * own_scale
    for coef in range(NCOEF):
        rows = pl.ds(coef * C, C)
        slope_ref[rows, :] = (
            upper_ref[rows, :]
            + slope_ref[rows, :] * own_scale
            - feat_ref[rows, :].astype(F32) * along
        )
    along = jnp.zeros((8, 2 * OWN), F32)
    for block in range(PER_GROUP):
        values = read_ghosts(low_ref, high_ref, block)
        along = along + fold_rows(ghost_slope_ref[pl.ds(block * C, C), :] * values)
    along = over_groups(along) * (1.0 / ROWS)
    along = along * ghost_scale * ghost_scale * ghost_scale
    for block in range(PER_GROUP):
        rows = pl.ds(block * C, C)
        values = read_ghosts(low_ref, high_ref, block)
        back = ghost_slope_ref[rows, :] * ghost_scale - values * along
        send_low_ref[rows, :] = back[:, :OWN].astype(BF16)
        send_high_ref[rows, :] = back[:, OWN:].astype(BF16)


def third_kernel(
    slope_ref, low_ref, high_ref, frame_ref, nb_ref, edge_ref, radial_ref, turned_ref,
    second_slope_ref, velocities_ref, masses_ref,
    tile_ref,
    wide_ref, gate_slope_ref, hidden_slope_ref,
):
    spread_frames(frame_ref, wide_ref)
    for group, rows in enumerate(GROUP_ROWS):
        block = pl.ds(group * PACKED, rows)
        back = jnp.concatenate([low_ref[pl.ds(0, rows), :], high_ref[pl.ds(0, rows), :]], axis=1)
        total = slope_ref[block, :] + dot(back, rim_place(group))
        hidden_slope_ref[block, :] = total * KNB ** (-0.5)

    @pl.loop(0, C // 16)
    def _(step):
        start = pl.multiple_of(step * 16, 16)
        gate_slopes = [None] * KNB
        for degree, row_count, offset in LAYOUT:
            slopes = [
                hidden_slope_ref[pl.ds((degree * degree + k) * C + start, 16), :]
                for k in range(2 * degree + 1)
            ]
            for slot in range(KNB):
                lanes = slot_lanes(slot)
                for row in range(row_count):
                    slope = slope_rows(
                        degree, row_count, offset, row, lanes, slopes, wide_ref
                    )
                    rows = pl.ds(edge_row(degree, row) * C + start, 16)
                    term = turned_ref[rows, lanes].astype(F32) * slope
                    before = gate_slopes[slot]
                    gate_slopes[slot] = term if before is None else before + term
        for slot in range(KNB):
            gate_slope_ref[pl.ds(start, 16), slot_lanes(slot)] = gate_slopes[slot]

    distance = edge_ref[3:4, :]
    slope = distance_slope(radial_ref, gate_slope_ref[...], distance) + second_slope_ref[0:1, :]
    vector = jnp.where(iota((8, EDGES), 0) < 3, edge_ref[...], 0.0)
    pull = vector * (slope / distance)
    virial = -jnp.sum(pull * vector)
    high, middle, low = split_three(pull)
    parts = jnp.concatenate([high, middle, low, jnp.zeros((8, EDGES), F32)], axis=0).astype(BF16)
    own_at, low_at, high_at = edge_sources(nb_ref)
    spread_own = jnp.transpose(own_one_hot(own_at).astype(F32)).astype(BF16)
    rim_at = jnp.where(low_at >= 0, low_at + (OWN - GHOST), high_at - OWN)
    rim_at = jnp.where((low_at >= 0) | (high_at >= 0), rim_at, -1)
    spread_rim = jnp.transpose(own_one_hot(rim_at).astype(F32)).astype(BF16)
    landed = dot(parts, spread_own)
    landed = landed[0:8] + landed[8:16] + landed[16:24]
    for slot in range(KNB):
        landed = landed - pull[:, slot * OWN : (slot + 1) * OWN]
    outward = dot(parts, spread_rim)
    outward = -(outward[0:8] + outward[8:16] + outward[16:24])
    masses = masses_ref[...]
    speed = jnp.concatenate([velocities_ref[...], jnp.zeros((5, OWN), F32)], axis=0)
    per_mass = STEP_TIME / masses
    kicked = speed - landed * per_mass
    lane = iota((8, OWN), 1)
    row = iota((8, OWN), 0)
    inner = (row < 3) & (lane >= GHOST) & (lane < OWN - GHOST)
    strain = virial + jnp.sum(jnp.where(inner, masses * kicked * kicked, 0.0))
    tile = jnp.where(row < 3, kicked, jnp.where(row == 3, per_mass, pltpu.roll(outward, 4, 0)))
    tile_ref[...] = jnp.where(row == 7, strain, tile)


def join_tiles(left, right):
    lane = iota((8, OWN), 1)
    row = iota((8, OWN), 0)
    top = lane >= OWN - GHOST
    rims = top | (lane < GHOST)
    near = jnp.where(top, left, right)
    pushed = pltpu.roll(jnp.where(top, right, left), 4, 0)
    per_mass = near[3:4]
    kicked = near + per_mass * pushed
    terms = jnp.where(rims & (row < 3), kicked * kicked * (STEP_TIME / per_mass), 0.0)
    return jnp.sum(terms)


def merge_runs(width, ways, tiles, caught):
    place = lax.axis_index("gx")
    lane = iota((8, OWN), 1)
    row = iota((8, OWN), 0)
    top = lane >= OWN - GHOST
    bottom = lane < GHOST
    digit = lax.rem(place // width, ways)
    at_start = lax.rem(place, width) == 0
    at_end = lax.rem(place, width) == width - 1
    ordered = []
    for run in range(ways):
        chosen = tiles[0]
        step = lax.rem(run - digit + ways, ways)
        for far in range(1, ways):
            chosen = jnp.where(step == far, tiles[far], chosen)
        ordered.append(chosen)
    merged = ordered[0]
    for run in range(1, ways):
        right = ordered[run]
        caught = jnp.where(top & (at_end & (digit == run - 1)), right, caught)
        caught = jnp.where(bottom & (at_start & (digit == run)), merged, caught)
        strain = merged + right + join_tiles(merged, right)
        outer = jnp.where(top == (row < 4), right, merged)
        merged = jnp.where(row == 7, strain, outer)
    return merged, caught


def merge_kernel(width, ways, *refs):
    ins, (tile_ref, caught_ref) = refs[:-2], refs[-2:]
    tiles = [ref[...] for ref in ins[:ways]]
    caught = ins[ways][...] if len(ins) > ways else jnp.zeros((8, OWN), F32)
    tile_ref[...], caught_ref[...] = merge_runs(width, ways, tiles, caught)


def finish_kernel(width, ways, first_round, *refs):
    (
        masses_ref, noise_ref, positions_ref, box_ref, control_ref,
        fractional_ref, velocities_ref, new_box_ref,
    ) = refs[-8:]
    tiles = [ref[...] for ref in refs[:ways]]
    start = tiles[0] if first_round else refs[ways][...]
    caught = jnp.zeros((8, OWN), F32) if first_round else refs[ways + 1][...]
    merged, caught = merge_runs(width, ways, tiles, caught)
    place = lax.axis_index("gx")
    lane = iota((8, OWN), 1)
    caught = jnp.where((lane >= OWN - GHOST) & (place == width * ways - 1), merged, caught)
    caught = jnp.where((lane < GHOST) & (place == 0), merged, caught)
    strain = merged[7:8] + join_tiles(merged, merged)
    kicked = (start + start[3:4] * pltpu.roll(caught, 4, 0))[0:3]
    row = iota((3, OWN), 0)
    box = jnp.where(row == 0, box_ref[0], jnp.where(row == 1, box_ref[1], box_ref[2]))
    volume = box_ref[0] * box_ref[1] * box_ref[2]
    pressure = strain / (3.0 * volume)
    rescale = jnp.exp(control_ref[1] * (pressure - control_ref[2]) / 3.0)
    kick = jnp.sqrt((1.0 - FRICTION * FRICTION) * control_ref[0] / masses_ref[...])
    thermal = FRICTION * kicked + kick * noise_ref[...]
    fractional_ref[...] = (positions_ref[...] + STEP_TIME * thermal) / box
    velocities_ref[...] = thermal / rescale
    scale = rescale[0, 0]
    for side in range(3):
        new_box_ref[side] = box_ref[side] * scale


SMALL = ("box", "control")


def call(kernel, outs, scratch, args, grant, layers=()):
    names = list(args)

    def body(*refs):
        views = list(refs)
        for name, layer in dict(layers).items():
            views[names.index(name)] = refs[names.index(name)].at[layer]
        kernel(*views)

    specs = []
    for name in names:
        if name in SMALL:
            specs.append(pl.BlockSpec(memory_space=pltpu.SMEM))
        else:
            specs.append(pl.BlockSpec(memory_space=pltpu.VMEM))
    out_specs = [
        pl.BlockSpec(memory_space=pltpu.SMEM if len(shape) == 1 else pltpu.VMEM)
        for shape, kind in outs
    ]
    return pl.pallas_call(
        body,
        out_shape=[jax.ShapeDtypeStruct(shape, kind) for shape, kind in outs],
        in_specs=specs,
        out_specs=out_specs,
        scratch_shapes=[pltpu.VMEM(shape, kind) for shape, kind in scratch],
        compiler_params=pltpu.CompilerParams(vmem_limit_bytes=grant << 20),
        cost_estimate=pl.CostEstimate(flops=0, bytes_accessed=1 << 20, transcendentals=0),
    )(*args.values())


def shards(
    node_feat,
    frames,
    neighbours,
    counts,
    positions,
    velocities,
    masses,
    thermal_noise,
    box_lengths,
    control,
    conv_weight,
    radial_weight,
    readout,
):
    assert positions.shape[1] == OWN
    count = lax.axis_size("gx")
    forward = [(i, (i + 1) % count) for i in range(count)]
    backward = [(target, source) for source, target in forward]

    def exchange(to_low, to_high):
        from_low = lax.ppermute(to_high, "gx", forward)
        from_high = lax.ppermute(to_low, "gx", backward)
        return from_low, from_high

    packed = ((PACKED, OWN), BF16)
    mass_row = masses[None, :]
    to_low, to_high = call(
        pack_kernel,
        [packed, packed],
        [((32, OWN), F32)],
        dict(feat=node_feat, positions=positions),
        8,
    )
    from_low, from_high = exchange(to_low, to_high)
    gathers = [((OWN, EDGES), BF16), ((GROUPS, 2 * OWN, EDGES), BF16)]
    work = [
        ((ROWS, OWN), BF16),
        ((PACKED, 2 * OWN), BF16),
        ((ROWS, EDGES), F32),
        ((WROWS, 8, EDGES), F32),
        ((EDGE_ROWS * C, EDGES), BF16),
        ((EDGE_ROWS * C, EDGES), F32),
        ((C, EDGES), F32),
        ((C, C), BF16),
        ((MMAX, 2 * C, 2 * C), BF16),
    ]
    hidden, turned, frame, edge, to_low, to_high = call(
        first_kernel,
        [
            ((ROWS, OWN), BF16),
            ((EDGE_ROWS * C, EDGES), BF16),
            ((WROWS, EDGES), F32),
            ((8, EDGES), F32),
            packed,
            packed,
        ],
        [((32, OWN), F32)] + gathers + work,
        dict(
            feat=node_feat, low=from_low, high=from_high, frames=frames,
            neighbours=neighbours, counts=counts[None, :], positions=positions,
            box=box_lengths, weight=conv_weight, radial=radial_weight,
        ),
        GRANTS[0],
        dict(weight=0, radial=0),
    )
    from_low, from_high = exchange(to_low, to_high)
    slope, second_slope, to_low, to_high = call(
        second_kernel,
        [((ROWS, OWN), F32), ((8, EDGES), F32), packed, packed],
        gathers
        + work
        + [
            ((ROWS, OWN), F32),
            ((C, EDGES), F32),
            ((EDGE_ROWS * C, EDGES), BF16),
            ((LMAX + 1, C, C), F32),
            ((ROWS, EDGES), BF16),
            ((PACKED, 2 * OWN), F32),
        ],
        dict(
            hidden=hidden, low=from_low, high=from_high, frame=frame, neighbours=neighbours,
            edge=edge, weight=conv_weight, radial=radial_weight, readout=readout,
        ),
        GRANTS[1],
        dict(weight=1, radial=1),
    )
    from_low, from_high = exchange(to_low, to_high)
    small = ((8, OWN), F32)
    (tile,) = call(
        third_kernel,
        [small],
        [((WROWS, 8, EDGES), F32), ((C, EDGES), F32), ((ROWS, OWN), F32)],
        dict(
            slope=slope, low=from_low, high=from_high, frame=frame, neighbours=neighbours,
            edge=edge, radial=radial_weight, turned=turned, second_slope=second_slope,
            velocities=velocities, masses=mass_row,
        ),
        GRANTS[2],
        dict(radial=0),
    )
    own = tile
    caught = None
    width = 1
    while True:
        left = count // width
        ways = next(way for way in (4, 2, 3, left) if left % way == 0)
        tiles = {"tile0": tile}
        for far in range(1, ways):
            pairs = []
            for target in range(count):
                digit = target // width % ways
                source = target + ((digit + far) % ways - digit) * width
                pairs.append((source, target))
            tiles["tile%d" % far] = lax.ppermute(tile, "gx", pairs)
        if caught is not None:
            tiles["caught"] = caught
        if width * ways == count:
            break
        tile, caught = call(
            functools.partial(merge_kernel, width, ways), [small, small], [], tiles, 1
        )
        width = width * ways
    if caught is not None:
        del tiles["caught"]
        tiles.update(own=own, caught=caught)
    return call(
        functools.partial(finish_kernel, width, ways, caught is None),
        [((3, OWN), F32), ((3, OWN), F32), ((3,), F32)],
        [],
        dict(
            tiles, masses=mass_row, noise=thermal_noise, positions=positions,
            box=box_lengths, control=control,
        ),
        1,
    )


def solution(mesh):
    return jax.shard_map(
        shards,
        mesh=mesh,
        in_specs=(
            P(None, ("groups", "gx")),
            P(None, ("groups", "gx")),
            P(None, ("groups", "gx")),
            P(("groups", "gx")),
            P(None, ("groups", "gx")),
            P(None, ("groups", "gx")),
            P(("groups", "gx")),
            P(None, ("groups", "gx")),
            P("groups"),
            P("groups"),
            P(),
            P(),
            P(),
        ),
        out_specs=(P(None, ("groups", "gx")), P(None, ("groups", "gx")), P("groups")),
        check_vma=False,
    )
```

```python
import functools

import jax
import jax.numpy as jnp
from jax import lax
from jax.experimental import pallas as pl
from jax.experimental.pallas import tpu as pltpu
from jax.sharding import PartitionSpec as P

LMAX = 4
MMAX = 2
NCOEF = 25
KNB = 4
GHOST = 32
NRBF = 16
C = 128
OWN = 128
ROWS = NCOEF * C
WROWS = 115
TILES = KNB // 2
EDGES = TILES * OWN

EPSILON = 1e-06
SOFTENING = 0.25
STEP_TIME = 0.1
FRICTION = 0.9
RADIAL_SPREAD = 0.5

GROUPS = OWN // GHOST
PER_GROUP = -(-NCOEF // GROUPS)
PACKED = PER_GROUP * C
LAST = (NCOEF - (GROUPS - 1) * PER_GROUP) * C
GROUP_ROWS = (PACKED,) * (GROUPS - 1) + (LAST,)
GRANT = 18

F32 = jnp.float32
BF16 = jnp.bfloat16


def frame_layout():
    layout = []
    offset = 0
    for degree in range(LMAX + 1):
        row_count = min(2 * degree + 1, 2 * MMAX + 1)
        layout.append((degree, row_count, offset))
        offset = offset + row_count * (2 * degree + 1)
    return layout


LAYOUT = frame_layout()
ORDER_START = (0, 5, 13)
EDGE_ROWS = 19


def edge_row(degree, row):
    if row == 0:
        return degree
    order = (row + 1) // 2
    return ORDER_START[order] + 2 * (degree - order) + (row + 1) % 2


def iota(shape, dim):
    return lax.broadcasted_iota(jnp.int32, shape, dim)


def dot(former, latter):
    return jnp.dot(former, latter, preferred_element_type=F32)


def one_hot(hit):
    return jnp.where(hit, 1.0, 0.0).astype(BF16)


def split_three(values):
    high = values.astype(BF16).astype(F32)
    rest = values - high
    middle = rest.astype(BF16).astype(F32)
    return high, middle, rest - middle


def rim_select(group):
    atom = iota((OWN, 2 * OWN), 0)
    lane = iota((OWN, 2 * OWN), 1)
    low = (lane < OWN) & (lane - GHOST * group == atom) & (atom < GHOST)
    high = (lane >= OWN) & (lane - OWN - GHOST * group == atom - (OWN - GHOST))
    return one_hot(low | (high & (atom >= OWN - GHOST)))


def rim_place(group):
    lane = iota((2 * OWN, OWN), 0)
    atom = iota((2 * OWN, OWN), 1)
    low = (lane < OWN) & (lane - GHOST * group == atom) & (atom < GHOST)
    high = (lane >= OWN) & (lane - OWN - GHOST * group == atom - (OWN - GHOST))
    return one_hot(low | (high & (atom >= OWN - GHOST)))


def pack_rims(read_rows, low_ref, high_ref, extra=None):
    selects = [rim_select(group) for group in range(GROUPS)]
    for block in range(PER_GROUP):
        total = None
        for group in range(GROUPS):
            coef = PER_GROUP * group + block
            if coef < NCOEF:
                part = dot(read_rows(coef * C, C), selects[group])
                total = part if total is None else total + part
        low_ref[pl.ds(block * C, C), :] = total[:, :OWN].astype(BF16)
        high_ref[pl.ds(block * C, C), :] = total[:, OWN:].astype(BF16)
        if extra is not None and block * C == LAST:
            rows = extra.shape[0]
            total = total[:rows] + dot(extra, selects[GROUPS - 1])
            low_ref[pl.ds(block * C, rows), :] = total[:, :OWN].astype(BF16)
            high_ref[pl.ds(block * C, rows), :] = total[:, OWN:].astype(BF16)


def position_parts(pos_ref, parts_ref):
    parts_ref[...] = jnp.zeros_like(parts_ref)
    for at, part in enumerate(split_three(pos_ref[...])):
        parts_ref[pl.ds(8 * at, 3), :] = part
    return parts_ref[...].astype(BF16)


def fetch(pairs, sems):
    copies = [
        pltpu.make_async_copy(source, target, sems.at[at])
        for at, (source, target) in enumerate(pairs)
    ]
    for copy in copies:
        copy.start()
    for copy in copies:
        copy.wait()


def pack_kernel(feat_hbm, pos_hbm, low_ref, high_ref, feat_ref, pos_ref, parts_ref, sems):
    fetch([(feat_hbm, feat_ref), (pos_hbm, pos_ref)], sems)
    parts = position_parts(pos_ref, parts_ref)
    pack_rims(lambda start, size: feat_ref[pl.ds(start, size), :], low_ref, high_ref, parts)


INNER = 0
RIM = 1


def inside(shape, half):
    lane = iota(shape, 1)
    middle = (lane >= GHOST) & (lane < OWN - GHOST)
    return middle if half == INNER else jnp.logical_not(middle)


def pick(even, odd, half):
    return jnp.where(inside(even.shape, half), even, pltpu.roll(odd, OWN // 2, 1))


def both_lanes(values, half):
    return pick(values, values, half)


def fold_slots(values):
    return values + pltpu.roll(values, OWN // 2, 1)


def slot_rows(ref, half):
    tiles = []
    for tile in range(TILES):
        even = jnp.broadcast_to(ref[2 * tile : 2 * tile + 1, :], (8, OWN))
        odd = jnp.broadcast_to(ref[2 * tile + 1 : 2 * tile + 2, :], (8, OWN))
        tiles.append(pick(even, odd, half)[:1])
    return tiles


def edge_atoms(half):
    return both_lanes(iota((8, OWN), 1), half)[:1]


def edge_sources(nb_ref, half):
    own_at = []
    low_at = []
    high_at = []
    for rows in slot_rows(nb_ref, half):
        place = jnp.bitwise_and(rows, OWN - 1)
        gap = place - edge_atoms(half)
        low = gap > OWN // 2
        high = gap < -(OWN // 2)
        own_at.append(jnp.where(low | high, -1, place))
        low_at.append(jnp.where(low, place - (OWN - GHOST), -1))
        high_at.append(jnp.where(high, place + OWN, -1))
    merge = functools.partial(jnp.concatenate, axis=1)
    return merge(own_at), merge(low_at), merge(high_at)


def own_one_hot(own_at):
    return one_hot(iota((OWN, EDGES), 0) == own_at)


def ghost_one_hot(low_at, high_at, group):
    at = jnp.maximum(low_at, high_at)
    at = jnp.where(at >= 0, at + GHOST * group, -1)
    return one_hot(iota((2 * OWN, EDGES), 0) == at)


def half_frames(frames_ref, counts, half, wide_ref):
    total = KNB * OWN
    column = iota((total, EDGES), 1)
    lane = jnp.bitwise_and(column, OWN - 1)
    middle = (lane >= GHOST) & (lane < OWN - GHOST)
    held = middle if half == INNER else jnp.logical_not(middle)
    atom = jnp.where(held, lane, jnp.bitwise_and(lane + OWN // 2, OWN - 1))
    slot = 2 * (column // OWN) + jnp.where(held, 0, 1)
    moved = dot(frames_ref[...], one_hot(iota((total, EDGES), 0) == atom * KNB + slot))
    counts = both_lanes(jnp.broadcast_to(counts, (8, OWN)), half)[:1]
    odd = jnp.where(inside((1, OWN), half), 0, 1)
    live = jnp.concatenate(
        [jnp.where(2 * tile + odd < counts, 1.0, 0.0) for tile in range(TILES)], axis=1
    )
    moved = moved * live
    for entry in range(WROWS):
        wide_ref[entry] = jnp.broadcast_to(moved[entry : entry + 1, :], (8, EDGES))


def corner_mask(block):
    lane = jnp.bitwise_and(iota((C, 2 * OWN), 1), OWN - 1)
    return (lane < OWN - GHOST) | (block * C < LAST)


def read_ghosts(low_ref, high_ref, block):
    low = low_ref[pl.ds(block * C, C), :].astype(F32)
    high = high_ref[pl.ds(block * C, C), :].astype(F32)
    merged = jnp.concatenate([low, high], axis=1)
    if block * C >= LAST:
        merged = jnp.where(corner_mask(block), merged, 0.0)
    return merged


def fold_rows(values):
    return jnp.sum(values.reshape(-1, 8, values.shape[1]), axis=0)


def over_groups(values):
    column = jnp.broadcast_to(jnp.sum(values, axis=0, keepdims=True), values.shape)
    sides = []
    for side in range(2):
        part = column[:, side * OWN : (side + 1) * OWN]
        total = part
        for group in range(1, GROUPS):
            total = total + pltpu.roll(part, GHOST * group, 1)
        sides.append(total)
    return jnp.concatenate(sides, axis=1)[:1]


def normalise_own(feat_ref, own_ref):
    squares = jnp.zeros((8, OWN), F32)
    for coef in range(NCOEF):
        block = feat_ref[pl.ds(coef * C, C), :].astype(F32)
        squares = squares + fold_rows(block * block)
    mean = jnp.sum(squares, axis=0, keepdims=True) * (1.0 / ROWS)
    scale = lax.rsqrt(mean + EPSILON)
    for coef in range(NCOEF):
        rows = pl.ds(coef * C, C)
        own_ref[rows, :] = (feat_ref[rows, :].astype(F32) * scale).astype(BF16)
    return scale


def normalise_ghosts(low_ref, high_ref, ghost_ref):
    squares = jnp.zeros((8, 2 * OWN), F32)
    for block in range(PER_GROUP):
        values = read_ghosts(low_ref, high_ref, block)
        squares = squares + fold_rows(values * values)
    scale = lax.rsqrt(over_groups(squares) * (1.0 / ROWS) + EPSILON)
    for block in range(PER_GROUP):
        values = read_ghosts(low_ref, high_ref, block) * scale
        ghost_ref[pl.ds(block * C, C), :] = values.astype(BF16)
    return scale


def gather(own_ref, own_hot_ref, out_ref, ghost_ref=None, ghost_hot_ref=None):
    for group, rows in enumerate(GROUP_ROWS):
        start = group * PACKED
        found = dot(own_ref[pl.ds(start, rows), :], own_hot_ref[...])
        if ghost_ref is not None:
            found = found + dot(ghost_ref[pl.ds(0, rows), :], ghost_hot_ref[group])
        out_ref[pl.ds(start, rows), :] = found


def twice(values):
    return jnp.concatenate([values, values], axis=0)


def slot_lanes(slot):
    return pl.ds(slot * OWN, OWN)


def to_frame(picked_ref, wide_ref, out_ref):
    @pl.loop(0, C // 16)
    def _(step):
        start = pl.multiple_of(step * 16, 16)
        for slot in range(TILES):
            lanes = slot_lanes(slot)
            for degree, row_count, offset in LAYOUT:
                size = 2 * degree + 1
                parts = [
                    picked_ref[pl.ds((degree * degree + k) * C + start, 16), lanes]
                    for k in range(size)
                ]
                for row in range(row_count):
                    total = None
                    for k in range(size):
                        term = twice(wide_ref[offset + row * size + k, :, lanes]) * parts[k]
                        total = term if total is None else total + term
                    at = edge_row(degree, row) * C
                    out_ref[pl.ds(at + start, 16), lanes] = total.astype(BF16)


def from_frame(frame_rows_ref, wide_ref, out_ref):
    @pl.loop(0, C // 16)
    def _(step):
        start = pl.multiple_of(step * 16, 16)
        for slot in range(TILES):
            lanes = slot_lanes(slot)
            for degree, row_count, offset in LAYOUT:
                size = 2 * degree + 1
                parts = [
                    frame_rows_ref[pl.ds(edge_row(degree, row) * C + start, 16), lanes]
                    for row in range(row_count)
                ]
                for k in range(size):
                    total = None
                    for row in range(row_count):
                        term = twice(wide_ref[offset + row * size + k, :, lanes]) * parts[row]
                        total = term if total is None else total + term
                    at = (degree * degree + k) * C
                    out_ref[pl.ds(at + start, 16), lanes] = total.astype(BF16)


def build_weights(weight_ref, layer, zero_ref, pair_ref):
    turned = [
        jnp.transpose(weight_ref[layer, part].astype(F32)).astype(BF16) for part in range(2 * MMAX + 1)
    ]
    zero_ref[...] = turned[0]
    for order in range(1, MMAX + 1):
        real, imag = turned[2 * order - 1], turned[2 * order]
        pair_ref[order - 1, :C, :C] = real
        pair_ref[order - 1, :C, C:] = -imag
        pair_ref[order - 1, C:, :C] = imag
        pair_ref[order - 1, C:, C:] = real


def build_back_weights(weight_ref, layer, zero_ref, pair_ref):
    zero_ref[...] = weight_ref[layer, 0]
    for order in range(1, MMAX + 1):
        real, imag = weight_ref[layer, 2 * order - 1], weight_ref[layer, 2 * order]
        pair_ref[order - 1, :C, :C] = real
        pair_ref[order - 1, :C, C:] = imag
        pair_ref[order - 1, C:, :C] = -imag
        pair_ref[order - 1, C:, C:] = real


def convolve(rows_ref, zero_ref, pair_ref, out_ref):
    for degree in range(LMAX + 1):
        rows = pl.ds(degree * C, C)
        out_ref[rows, :] = dot(zero_ref[...], rows_ref[rows, :]).astype(out_ref.dtype)
    for order in range(1, MMAX + 1):
        for degree in range(order, LMAX + 1):
            rows = pl.ds((ORDER_START[order] + 2 * (degree - order)) * C, 2 * C)
            out_ref[rows, :] = dot(pair_ref[order - 1], rows_ref[rows, :]).astype(out_ref.dtype)


def radial(distance):
    centers = 0.5 + 5.5 * iota((NRBF, EDGES), 0).astype(F32) / (NRBF - 1)
    offset = (distance - centers) / RADIAL_SPREAD
    return jnp.exp(-(offset * offset)), offset


def edge_gate(radial_ref, basis):
    return lax.dot_general(
        radial_ref[...],
        basis,
        (((0,), (0,)), ((), ())),
        precision=lax.Precision.HIGHEST,
        preferred_element_type=F32,
    )


def distance_slope(radial_ref, gate_slope, distance):
    basis, offset = radial(distance)
    basis_slope = jnp.dot(
        radial_ref[...], gate_slope, precision=lax.Precision.HIGHEST, preferred_element_type=F32
    )
    terms = basis_slope * basis * offset * (-2.0 / RADIAL_SPREAD)
    return jnp.sum(terms, axis=0, keepdims=True)


def message_rows(degree, row_count, offset, start, turned_ref, gate_ref, wide_ref):
    size = 2 * degree + 1
    sums = [None] * size
    for slot in range(TILES):
        lanes = slot_lanes(slot)
        gate = gate_ref[pl.ds(start, 16), lanes]
        for row in range(row_count):
            gated = turned_ref[pl.ds(edge_row(degree, row) * C + start, 16), lanes] * gate
            for k in range(size):
                term = twice(wide_ref[offset + row * size + k, :, lanes]) * gated
                sums[k] = term if sums[k] is None else sums[k] + term
    return [fold_slots(total) for total in sums]


def slope_rows(degree, row_count, offset, row, lanes, slopes, wide_ref):
    size = 2 * degree + 1
    total = None
    for k in range(size):
        term = twice(wide_ref[offset + row * size + k, :, lanes]) * slopes[k]
        total = term if total is None else total + term
    return total


def layer_forward(picked_ref, wide_ref, rows_ref, zero_ref, pair_ref, turned_ref):
    to_frame(picked_ref, wide_ref, rows_ref)
    convolve(rows_ref, zero_ref, pair_ref, turned_ref)


def add_messages(base_ref, half, turned_ref, gate_ref, wide_ref, hidden_ref, keep_ref):
    @pl.loop(0, C // 16)
    def _(step):
        start = pl.multiple_of(step * 16, 16)
        held = inside((16, OWN), half)
        for degree, row_count, offset in LAYOUT:
            sums = message_rows(degree, row_count, offset, start, turned_ref, gate_ref, wide_ref)
            for k, total in enumerate(sums):
                rows = pl.ds((degree * degree + k) * C + start, 16)
                added = jnp.where(held, total * KNB ** (-0.5), 0.0)
                hidden_ref[rows, :] = (base_ref[rows, :].astype(F32) + added).astype(BF16)
        for row in range(EDGE_ROWS):
            rows = pl.ds(row * C + start, 16)
            keep_ref[rows, :] = turned_ref[rows, :].astype(BF16)


def edge_geometry(source, shift, target, edge_ref):
    first = iota((8, EDGES), 0) == 0
    if shift is not None:
        source = source + jnp.where(first, shift, 0.0)
    vector = source - target
    distance = jnp.sqrt(jnp.sum(vector * vector, axis=0, keepdims=True) + SOFTENING)
    edge_ref[...] = jnp.where(iota((8, EDGES), 0) == 3, distance, vector)
    return distance


def join_parts(found):
    return (found[0:8] + found[8:16]) + found[16:24]


def first_inner_kernel(
    feat_hbm, frames_hbm, nb_hbm, counts_hbm, pos_hbm, box_hbm, weight_hbm, radial_hbm,
    readout_hbm,
    hidden_ref, keep_ref, edge_ref, own_ref, inner_wide_ref, rim_wide_ref, inner_hot_ref,
    rim_hot_ref, ghost_hot_ref, index_ref, target_ref, parts_out_ref, zero_ref, pair_ref,
    radial_ref, readout_wide_ref,
    feat_ref, frames_ref, nb_ref, counts_ref, pos_ref, box_ref, weight_ref, readout_ref,
    parts_ref, picked_ref, rows_ref, turned_ref, gate_ref, sems,
):
    fetch(
        [
            (nb_hbm, nb_ref), (counts_hbm, counts_ref), (pos_hbm, pos_ref),
            (box_hbm, box_ref), (frames_hbm, frames_ref), (radial_hbm, radial_ref),
            (feat_hbm, feat_ref), (weight_hbm, weight_ref), (readout_hbm, readout_ref),
        ],
        sems,
    )
    counts = counts_ref[...]
    half_frames(frames_ref, counts, INNER, inner_wide_ref)
    own_at, low_at, high_at = edge_sources(nb_ref, INNER)
    index_ref[...] = jnp.full((8, 2 * EDGES), -1, jnp.int32)
    index_ref[0:1, :EDGES] = own_at
    inner_hot_ref[...] = own_one_hot(own_at)
    parts = position_parts(pos_ref, parts_ref)
    parts_out_ref[...] = parts
    parts_ref[pl.ds(0, 3), :] = pos_ref[...]
    positions = parts_ref[0:8, :]
    target = jnp.concatenate([both_lanes(positions, INNER)] * TILES, axis=1)
    distance = edge_geometry(join_parts(dot(parts, inner_hot_ref[...])), None, target, edge_ref)
    gate_ref[...] = edge_gate(radial_ref.at[0], radial(distance)[0])
    build_weights(weight_ref, 0, zero_ref.at[0], pair_ref.at[0])
    normalise_own(feat_ref, own_ref)
    gather(own_ref, inner_hot_ref, picked_ref)
    layer_forward(
        picked_ref, inner_wide_ref, rows_ref, zero_ref.at[0], pair_ref.at[0], turned_ref
    )
    add_messages(feat_ref, INNER, turned_ref, gate_ref, inner_wide_ref, hidden_ref, keep_ref)
    half_frames(frames_ref, counts, RIM, rim_wide_ref)
    own_at, low_at, high_at = edge_sources(nb_ref, RIM)
    index_ref[0:1, EDGES:] = own_at
    index_ref[1:2, EDGES:] = low_at
    index_ref[2:3, EDGES:] = high_at
    rim_hot_ref[...] = own_one_hot(own_at)
    for group in range(GROUPS):
        ghost_hot_ref[group] = ghost_one_hot(low_at, high_at, group)
    place = lax.axis_index("gx")
    low_shift = jnp.where(place == 0, -box_ref[0], 0.0)
    high_shift = jnp.where(place == lax.axis_size("gx") - 1, box_ref[0], 0.0)
    shift = jnp.where(low_at >= 0, low_shift, jnp.where(high_at >= 0, high_shift, 0.0))
    target = jnp.concatenate([both_lanes(positions, RIM)] * TILES, axis=1)
    target_ref[...] = jnp.where(iota((8, EDGES), 0) == 3, shift, target)
    build_weights(weight_ref, 1, zero_ref.at[1], pair_ref.at[1])
    build_back_weights(weight_ref, 1, zero_ref.at[2], pair_ref.at[2])
    for degree in range(LMAX + 1):
        row = jnp.broadcast_to(readout_ref[degree : degree + 1, :], (C, C))
        readout_wide_ref[degree] = jnp.transpose(row) * (1.0 / (2 * degree + 1))


def first_rim_kernel(
    base_ref, low_ref, high_ref, own_ref, wide_ref, own_hot_ref, ghost_hot_ref, target_ref,
    parts_ref, zero_ref, pair_ref, radial_ref,
    hidden_ref, keep_ref, edge_ref, send_low_ref, send_high_ref,
    ghost_ref, picked_ref, rows_ref, turned_ref, gate_ref,
):
    ghosts = jnp.concatenate(
        [low_ref[pl.ds(LAST, 32), :], high_ref[pl.ds(LAST, 32), :]], axis=1
    )
    found = dot(parts_ref[...], own_hot_ref[...]) + dot(ghosts, ghost_hot_ref[GROUPS - 1])
    target = jnp.where(iota((8, EDGES), 0) == 3, 0.0, target_ref[...])
    distance = edge_geometry(join_parts(found), target_ref[3:4, :], target, edge_ref)
    gate_ref[...] = edge_gate(radial_ref.at[0], radial(distance)[0])
    normalise_ghosts(low_ref, high_ref, ghost_ref)
    gather(own_ref, own_hot_ref, picked_ref, ghost_ref, ghost_hot_ref)
    layer_forward(picked_ref, wide_ref, rows_ref, zero_ref.at[0], pair_ref.at[0], turned_ref)
    add_messages(base_ref, RIM, turned_ref, gate_ref, wide_ref, hidden_ref, keep_ref)
    pack_rims(lambda start, size: hidden_ref[pl.ds(start, size), :], send_low_ref, send_high_ref)


def turn_slopes(
    hidden_ref, half, turned_ref, gate_ref, wide_ref, readout_wide_ref, upper_ref,
    turned_slope_ref, gate_slope_ref,
):
    @pl.loop(0, C // 16)
    def _(step):
        start = pl.multiple_of(step * 16, 16)
        channels = pl.ds(start, 16)
        gate_slopes = [None] * TILES
        for degree, row_count, offset in LAYOUT:
            sums = message_rows(degree, row_count, offset, start, turned_ref, gate_ref, wide_ref)
            weight = readout_wide_ref[degree, channels, :]
            slopes = []
            for k, total in enumerate(sums):
                rows = pl.ds((degree * degree + k) * C + start, 16)
                below = both_lanes(hidden_ref[rows, :].astype(F32), half)
                slope = (below + total * KNB ** (-0.5)) * weight
                upper_ref[rows, :] = slope * 2.0
                slopes.append(slope * (2.0 * KNB ** (-0.5)))
            for slot in range(TILES):
                lanes = slot_lanes(slot)
                gate = gate_ref[channels, lanes]
                for row in range(row_count):
                    slope = slope_rows(
                        degree, row_count, offset, row, lanes, slopes, wide_ref
                    )
                    rows = pl.ds(edge_row(degree, row) * C + start, 16)
                    term = turned_ref[rows, lanes] * slope
                    before = gate_slopes[slot]
                    gate_slopes[slot] = term if before is None else before + term
                    turned_slope_ref[rows, lanes] = (slope * gate).astype(BF16)
        for slot in range(TILES):
            gate_slope_ref[channels, slot_lanes(slot)] = gate_slopes[slot]


def write_distance_slope(radial_ref, gate_slope_ref, distance, out_ref):
    slope = distance_slope(radial_ref, gate_slope_ref[...], distance)
    out_ref[...] = jnp.broadcast_to(slope, (8, EDGES))


def second_inner_kernel(
    hidden_ref, wide_ref, own_hot_ref, edge_ref, zero_ref, pair_ref, radial_ref,
    readout_wide_ref,
    own_ref, scale_ref, upper_ref, turned_slope_ref, slope_ref,
    picked_ref, rows_ref, turned_ref, gate_ref, gate_slope_ref,
):
    distance = edge_ref[3:4, :]
    gate_ref[...] = edge_gate(radial_ref.at[1], radial(distance)[0])
    scale_ref[...] = jnp.broadcast_to(normalise_own(hidden_ref, own_ref), (8, OWN))
    gather(own_ref, own_hot_ref, picked_ref)
    layer_forward(picked_ref, wide_ref, rows_ref, zero_ref.at[1], pair_ref.at[1], turned_ref)
    turn_slopes(
        hidden_ref, INNER, turned_ref, gate_ref, wide_ref, readout_wide_ref, upper_ref,
        turned_slope_ref, gate_slope_ref,
    )
    write_distance_slope(radial_ref.at[1], gate_slope_ref, distance, slope_ref)


def scatter_own(edge_slope_ref, own_hot_ref, out_ref, add_ref=None):
    spread = jnp.transpose(own_hot_ref[...].astype(F32)).astype(BF16)
    for group, rows in enumerate(GROUP_ROWS):
        block = pl.ds(group * PACKED, rows)
        part = dot(edge_slope_ref[block, :], spread)
        out_ref[block, :] = part if add_ref is None else part + add_ref[block, :]


def second_rim_kernel(
    hidden_ref, low_ref, high_ref, own_ref, wide_ref, own_hot_ref, ghost_hot_ref, edge_ref,
    zero_ref, pair_ref, radial_ref, readout_wide_ref,
    upper_ref, slope_ref, own_slope_ref, send_low_ref, send_high_ref,
    ghost_ref, picked_ref, rows_ref, turned_ref, gate_ref, gate_slope_ref, turned_slope_ref,
    edge_slope_ref, ghost_slope_ref,
):
    distance = edge_ref[3:4, :]
    gate_ref[...] = edge_gate(radial_ref.at[1], radial(distance)[0])
    ghost_scale = normalise_ghosts(low_ref, high_ref, ghost_ref)
    gather(own_ref, own_hot_ref, picked_ref, ghost_ref, ghost_hot_ref)
    layer_forward(picked_ref, wide_ref, rows_ref, zero_ref.at[1], pair_ref.at[1], turned_ref)
    turn_slopes(
        hidden_ref, RIM, turned_ref, gate_ref, wide_ref, readout_wide_ref, upper_ref,
        turned_slope_ref, gate_slope_ref,
    )
    convolve(turned_slope_ref, zero_ref.at[2], pair_ref.at[2], turned_ref)
    from_frame(turned_ref, wide_ref, edge_slope_ref)
    for group, rows in enumerate(GROUP_ROWS):
        spread_ghost = jnp.transpose(ghost_hot_ref[group].astype(F32)).astype(BF16)
        part = dot(edge_slope_ref[pl.ds(group * PACKED, rows), :], spread_ghost)
        if group == 0:
            ghost_slope_ref[...] = part
        else:
            ghost_slope_ref[pl.ds(0, rows), :] += part
    along = jnp.zeros((8, 2 * OWN), F32)
    for block in range(PER_GROUP):
        values = read_ghosts(low_ref, high_ref, block)
        along = along + fold_rows(ghost_slope_ref[pl.ds(block * C, C), :] * values)
    along = over_groups(along) * (1.0 / ROWS)
    along = along * ghost_scale * ghost_scale * ghost_scale
    for block in range(PER_GROUP):
        rows = pl.ds(block * C, C)
        values = read_ghosts(low_ref, high_ref, block)
        back = ghost_slope_ref[rows, :] * ghost_scale - values * along
        send_low_ref[rows, :] = back[:, :OWN].astype(BF16)
        send_high_ref[rows, :] = back[:, OWN:].astype(BF16)
    scatter_own(edge_slope_ref, own_hot_ref, own_slope_ref)
    write_distance_slope(radial_ref.at[1], gate_slope_ref, distance, slope_ref)


def gate_slopes_back(hidden_slope_ref, half, wide_ref, keep_ref, gate_slope_ref):
    @pl.loop(0, C // 16)
    def _(step):
        start = pl.multiple_of(step * 16, 16)
        gate_slopes = [None] * TILES
        for degree, row_count, offset in LAYOUT:
            slopes = [
                both_lanes(
                    hidden_slope_ref[pl.ds((degree * degree + k) * C + start, 16), :], half
                )
                for k in range(2 * degree + 1)
            ]
            for slot in range(TILES):
                lanes = slot_lanes(slot)
                for row in range(row_count):
                    slope = slope_rows(
                        degree, row_count, offset, row, lanes, slopes, wide_ref
                    )
                    rows = pl.ds(edge_row(degree, row) * C + start, 16)
                    term = keep_ref[rows, lanes].astype(F32) * slope
                    before = gate_slopes[slot]
                    gate_slopes[slot] = term if before is None else before + term
        for slot in range(TILES):
            gate_slope_ref[pl.ds(start, 16), slot_lanes(slot)] = gate_slopes[slot]


def edge_pulls(radial_ref, gate_slope_ref, edge_ref, second_slope_ref, half):
    distance = edge_ref[3:4, :]
    slope = distance_slope(radial_ref, gate_slope_ref[...], distance) + second_slope_ref[0:1, :]
    vector = jnp.where(iota((8, EDGES), 0) < 3, edge_ref[...], 0.0)
    pull = vector * (slope / distance)
    virial = -jnp.sum(pull * vector)
    high, middle, low = split_three(pull)
    parts = jnp.concatenate([high, middle, low, jnp.zeros((8, EDGES), F32)], axis=0).astype(BF16)
    on_target = pull[:, :OWN]
    for tile in range(1, TILES):
        on_target = on_target + pull[:, tile * OWN : (tile + 1) * OWN]
    on_target = jnp.where(inside((8, OWN), half), fold_slots(on_target), 0.0)
    return parts, on_target, virial


def spread(hot):
    return jnp.transpose(hot.astype(F32)).astype(BF16)


def middle_kernel(
    hidden_ref, scale_ref, inner_upper_ref, rim_upper_ref, own_slope_ref, turned_slope_ref,
    wide_ref, own_hot_ref, zero_ref, pair_ref, radial_ref, keep_ref, edge_ref,
    second_slope_ref,
    slope_ref, part_ref,
    turned_ref, edge_slope_ref, gate_slope_ref,
):
    convolve(turned_slope_ref, zero_ref.at[2], pair_ref.at[2], turned_ref)
    from_frame(turned_ref, wide_ref, edge_slope_ref)
    scatter_own(edge_slope_ref, own_hot_ref, slope_ref, own_slope_ref)
    scale = scale_ref[0:1, :]
    along = jnp.zeros((8, OWN), F32)
    for coef in range(NCOEF):
        rows = pl.ds(coef * C, C)
        along = along + fold_rows(slope_ref[rows, :] * hidden_ref[rows, :].astype(F32))
    along = jnp.sum(along, axis=0, keepdims=True) * (1.0 / ROWS)
    along = along * scale * scale * scale
    held = inside((C, OWN), INNER)
    for coef in range(NCOEF):
        rows = pl.ds(coef * C, C)
        upper = jnp.where(held, inner_upper_ref[rows, :], rim_upper_ref[rows, :])
        total = upper + slope_ref[rows, :] * scale - hidden_ref[rows, :].astype(F32) * along
        slope_ref[rows, :] = total * KNB ** (-0.5)
    gate_slopes_back(slope_ref, INNER, wide_ref, keep_ref, gate_slope_ref)
    parts, on_target, virial = edge_pulls(
        radial_ref.at[0], gate_slope_ref, edge_ref, second_slope_ref, INNER
    )
    landed = join_parts(dot(parts, spread(own_hot_ref[...]))) - on_target
    part_ref[...] = jnp.where(iota((8, OWN), 0) == 7, virial, landed)


def last_kernel(
    slope_ref, low_ref, high_ref, wide_ref, own_hot_ref, index_ref, radial_ref, keep_ref,
    edge_ref, second_slope_ref, part_ref, velocities_ref, masses_ref,
    tile_ref,
    gate_slope_ref, hidden_slope_ref,
):
    for group, rows in enumerate(GROUP_ROWS):
        block = pl.ds(group * PACKED, rows)
        back = jnp.concatenate([low_ref[pl.ds(0, rows), :], high_ref[pl.ds(0, rows), :]], axis=1)
        added = dot(back, rim_place(group)) * KNB ** (-0.5)
        hidden_slope_ref[block, :] = slope_ref[block, :] + added
    gate_slopes_back(hidden_slope_ref, RIM, wide_ref, keep_ref, gate_slope_ref)
    parts, on_target, virial = edge_pulls(
        radial_ref.at[0], gate_slope_ref, edge_ref, second_slope_ref, RIM
    )
    landed = join_parts(dot(parts, spread(own_hot_ref[...]))) - on_target + part_ref[...]
    low_at, high_at = index_ref[1:2, EDGES:], index_ref[2:3, EDGES:]
    rim_at = jnp.where(low_at >= 0, low_at + (OWN - GHOST), high_at - OWN)
    rim_at = jnp.where((low_at >= 0) | (high_at >= 0), rim_at, -1)
    outward = -join_parts(dot(parts, spread(own_one_hot(rim_at))))
    virial = virial + part_ref[7:8, :]
    masses = masses_ref[...]
    speed = jnp.concatenate([velocities_ref[...], jnp.zeros((5, OWN), F32)], axis=0)
    per_mass = STEP_TIME / masses
    kicked = speed - landed * per_mass
    lane = iota((8, OWN), 1)
    row = iota((8, OWN), 0)
    inner = (row < 3) & (lane >= GHOST) & (lane < OWN - GHOST)
    strain = virial + jnp.sum(jnp.where(inner, masses * kicked * kicked, 0.0))
    tile = jnp.where(row < 3, kicked, jnp.where(row == 3, per_mass, pltpu.roll(outward, 4, 0)))
    tile_ref[...] = jnp.where(row == 7, strain, tile)


def join_tiles(left, right):
    lane = iota((8, OWN), 1)
    row = iota((8, OWN), 0)
    top = lane >= OWN - GHOST
    rims = top | (lane < GHOST)
    near = jnp.where(top, left, right)
    pushed = pltpu.roll(jnp.where(top, right, left), 4, 0)
    per_mass = near[3:4]
    kicked = near + per_mass * pushed
    terms = jnp.where(rims & (row < 3), kicked * kicked * (STEP_TIME / per_mass), 0.0)
    return jnp.sum(terms)


def merge_runs(width, ways, tiles, caught):
    place = lax.axis_index("gx")
    lane = iota((8, OWN), 1)
    row = iota((8, OWN), 0)
    top = lane >= OWN - GHOST
    bottom = lane < GHOST
    digit = lax.rem(place // width, ways)
    at_start = lax.rem(place, width) == 0
    at_end = lax.rem(place, width) == width - 1
    ordered = []
    for run in range(ways):
        chosen = tiles[0]
        step = lax.rem(run - digit + ways, ways)
        for far in range(1, ways):
            chosen = jnp.where(step == far, tiles[far], chosen)
        ordered.append(chosen)
    merged = ordered[0]
    for run in range(1, ways):
        right = ordered[run]
        caught = jnp.where(top & (at_end & (digit == run - 1)), right, caught)
        caught = jnp.where(bottom & (at_start & (digit == run)), merged, caught)
        strain = merged + right + join_tiles(merged, right)
        outer = jnp.where(top == (row < 4), right, merged)
        merged = jnp.where(row == 7, strain, outer)
    return merged, caught


def merge_kernel(width, ways, *refs):
    ins, (tile_ref, caught_ref) = refs[:-2], refs[-2:]
    tiles = [ref[...] for ref in ins[:ways]]
    caught = ins[ways][...] if len(ins) > ways else jnp.zeros((8, OWN), F32)
    tile_ref[...], caught_ref[...] = merge_runs(width, ways, tiles, caught)


def finish_kernel(width, ways, first_round, *refs):
    (
        masses_ref, noise_ref, positions_ref, box_ref, control_ref,
        fractional_ref, velocities_ref, new_box_ref,
    ) = refs[-8:]
    tiles = [ref[...] for ref in refs[:ways]]
    start = tiles[0] if first_round else refs[ways][...]
    caught = jnp.zeros((8, OWN), F32) if first_round else refs[ways + 1][...]
    merged, caught = merge_runs(width, ways, tiles, caught)
    place = lax.axis_index("gx")
    lane = iota((8, OWN), 1)
    caught = jnp.where((lane >= OWN - GHOST) & (place == width * ways - 1), merged, caught)
    caught = jnp.where((lane < GHOST) & (place == 0), merged, caught)
    strain = merged[7:8] + join_tiles(merged, merged)
    kicked = (start + start[3:4] * pltpu.roll(caught, 4, 0))[0:3]
    row = iota((3, OWN), 0)
    box = jnp.where(row == 0, box_ref[0], jnp.where(row == 1, box_ref[1], box_ref[2]))
    volume = box_ref[0] * box_ref[1] * box_ref[2]
    pressure = strain / (3.0 * volume)
    rescale = jnp.exp(control_ref[1] * (pressure - control_ref[2]) / 3.0)
    kick = jnp.sqrt((1.0 - FRICTION * FRICTION) * control_ref[0] / masses_ref[...])
    thermal = FRICTION * kicked + kick * noise_ref[...]
    fractional_ref[...] = (positions_ref[...] + STEP_TIME * thermal) / box
    velocities_ref[...] = thermal / rescale
    scale = rescale[0, 0]
    for side in range(3):
        new_box_ref[side] = box_ref[side] * scale


SMALL = ("box", "control")


def call(kernel, outs, scratch, args, grant=GRANT, hbm=False, cost=1):
    def space(name):
        if hbm:
            return pltpu.HBM
        return pltpu.SMEM if name in SMALL else pltpu.VMEM

    def buffer(entry):
        return entry if len(entry) == 3 else entry + (pltpu.VMEM,)

    buffers = []
    for entry in scratch:
        if isinstance(entry, int):
            buffers.append(pltpu.SemaphoreType.DMA((entry,)))
        else:
            shape, kind, where = buffer(entry)
            buffers.append(where(shape, kind))
    return pl.pallas_call(
        kernel,
        out_shape=[jax.ShapeDtypeStruct(shape, kind) for shape, kind in outs],
        in_specs=[pl.BlockSpec(memory_space=space(name)) for name in args],
        out_specs=[
            pl.BlockSpec(memory_space=pltpu.SMEM if len(shape) == 1 else pltpu.VMEM)
            for shape, kind in outs
        ],
        scratch_shapes=buffers,
        compiler_params=pltpu.CompilerParams(vmem_limit_bytes=grant << 20),
        cost_estimate=pl.CostEstimate(
            flops=cost << 30, bytes_accessed=1 << 20, transcendentals=0
        ),
    )(*args.values())


def shards(
    node_feat,
    frames,
    neighbours,
    counts,
    positions,
    velocities,
    masses,
    thermal_noise,
    box_lengths,
    control,
    conv_weight,
    radial_weight,
    readout,
):
    assert positions.shape[1] == OWN
    count = lax.axis_size("gx")
    forward = [(i, (i + 1) % count) for i in range(count)]
    backward = [(target, source) for source, target in forward]

    def exchange(to_low, to_high):
        from_low = lax.ppermute(to_high, "gx", forward)
        from_high = lax.ppermute(to_low, "gx", backward)
        return from_low, from_high

    packed = ((PACKED, OWN), BF16)
    own_rows = ((ROWS, OWN), BF16)
    own_sums = ((ROWS, OWN), F32)
    kept = ((EDGE_ROWS * C, EDGES), BF16)
    turned = ((EDGE_ROWS * C, EDGES), F32)
    picked = ((ROWS, EDGES), F32)
    edge = ((8, EDGES), F32)
    wide = ((WROWS, 8, EDGES), F32)
    gate = ((C, EDGES), F32)
    hot = ((OWN, EDGES), BF16)
    ghost = ((PACKED, 2 * OWN), BF16)
    small = ((8, OWN), F32)
    place = ((3, OWN), F32)
    parts = ((32, OWN), F32)
    mass_row = masses[None, :]
    to_low, to_high = call(
        pack_kernel,
        [packed, packed],
        [own_rows, place, parts, 2],
        dict(feat=node_feat, positions=positions),
        grant=8,
        hbm=True,
    )
    from_low, from_high = exchange(to_low, to_high)
    (
        hidden, keep_inner, edge_inner, own, wide_inner, wide_rim, hot_inner, hot_rim,
        hot_ghost, index, target, own_parts, zero, pair, radial_rows, readout_wide,
    ) = call(
        first_inner_kernel,
        [
            own_rows, kept, edge, own_rows, wide, wide, hot, hot,
            ((GROUPS, 2 * OWN, EDGES), BF16), ((8, 2 * EDGES), jnp.int32), edge,
            ((32, OWN), BF16), ((3, C, C), BF16), ((3, MMAX, 2 * C, 2 * C), BF16),
            (radial_weight.shape, F32), ((LMAX + 1, C, C), F32),
        ],
        [
            own_rows, (frames.shape, BF16), ((KNB, OWN), jnp.int32), ((1, OWN), jnp.int32),
            place, ((3,), F32, pltpu.SMEM), (conv_weight.shape, BF16), (readout.shape, F32),
            parts, picked, kept, turned, gate, 9,
        ],
        dict(
            feat=node_feat, frames=frames, neighbours=neighbours, counts=counts[None, :],
            positions=positions, box=box_lengths, weight=conv_weight, radial=radial_weight,
            readout=readout,
        ),
        hbm=True,
        cost=5,
    )
    hidden, keep_rim, edge_rim, to_low, to_high = call(
        first_rim_kernel,
        [own_rows, kept, edge, packed, packed],
        [ghost, picked, kept, turned, gate],
        dict(
            base=hidden, low=from_low, high=from_high, own=own, wide=wide_rim, hot=hot_rim,
            ghost_hot=hot_ghost, target=target, parts=own_parts, zero=zero, pair=pair,
            radial=radial_rows,
        ),
    )
    from_low, from_high = exchange(to_low, to_high)
    own, scale, upper_inner, turned_slope, slope_inner = call(
        second_inner_kernel,
        [own_rows, small, own_sums, kept, edge],
        [picked, kept, turned, gate, gate],
        dict(
            hidden=hidden, wide=wide_inner, hot=hot_inner, edge=edge_inner, zero=zero,
            pair=pair, radial=radial_rows, readout=readout_wide,
        ),
        cost=5,
    )
    upper_rim, slope_rim, own_slope, to_low, to_high = call(
        second_rim_kernel,
        [own_sums, edge, own_sums, packed, packed],
        [
            ghost, picked, kept, turned, gate, gate, kept, ((ROWS, EDGES), BF16),
            ((PACKED, 2 * OWN), F32),
        ],
        dict(
            hidden=hidden, low=from_low, high=from_high, own=own, wide=wide_rim, hot=hot_rim,
            ghost_hot=hot_ghost, edge=edge_rim, zero=zero, pair=pair, radial=radial_rows,
            readout=readout_wide,
        ),
    )
    from_low, from_high = exchange(to_low, to_high)
    slope, part = call(
        middle_kernel,
        [own_sums, small],
        [turned, ((ROWS, EDGES), BF16), gate],
        dict(
            hidden=hidden, scale=scale, upper_inner=upper_inner, upper_rim=upper_rim,
            own_slope=own_slope, turned_slope=turned_slope, wide=wide_inner, hot=hot_inner,
            zero=zero, pair=pair, radial=radial_rows, keep=keep_inner, edge=edge_inner,
            second_slope=slope_inner,
        ),
        cost=5,
    )
    (tile,) = call(
        last_kernel,
        [small],
        [gate, own_sums],
        dict(
            slope=slope, low=from_low, high=from_high, wide=wide_rim, hot=hot_rim, index=index,
            radial=radial_rows, keep=keep_rim, edge=edge_rim, second_slope=slope_rim,
            part=part, velocities=velocities, masses=mass_row,
        ),
    )
    own = tile
    caught = None
    width = 1
    while True:
        left = count // width
        ways = next(way for way in (4, 2, 3, left) if left % way == 0)
        tiles = {"tile0": tile}
        for far in range(1, ways):
            pairs = []
            for target in range(count):
                digit = target // width % ways
                source = target + ((digit + far) % ways - digit) * width
                pairs.append((source, target))
            tiles["tile%d" % far] = lax.ppermute(tile, "gx", pairs)
        if caught is not None:
            tiles["caught"] = caught
        if width * ways == count:
            break
        tile, caught = call(
            functools.partial(merge_kernel, width, ways), [small, small], [], tiles, grant=1
        )
        width = width * ways
    if caught is not None:
        del tiles["caught"]
        tiles.update(own=own, caught=caught)
    return call(
        functools.partial(finish_kernel, width, ways, caught is None),
        [((3, OWN), F32), ((3, OWN), F32), ((3,), F32)],
        [],
        dict(
            tiles, masses=mass_row, noise=thermal_noise, positions=positions,
            box=box_lengths, control=control,
        ),
        grant=1,
    )


def solution(mesh):
    return jax.shard_map(
        shards,
        mesh=mesh,
        in_specs=(
            P(None, ("groups", "gx")),
            P(None, ("groups", "gx")),
            P(None, ("groups", "gx")),
            P(("groups", "gx")),
            P(None, ("groups", "gx")),
            P(None, ("groups", "gx")),
            P(("groups", "gx")),
            P(None, ("groups", "gx")),
            P("groups"),
            P("groups"),
            P(),
            P(),
            P(),
        ),
        out_specs=(P(None, ("groups", "gx")), P(None, ("groups", "gx")), P("groups")),
        check_vma=False,
    )
```

```python
import functools

import jax
import jax.numpy as jnp
from jax import lax
from jax.experimental import pallas as pl
from jax.experimental.pallas import tpu as pltpu
from jax.sharding import PartitionSpec as P

LMAX = 4
MMAX = 2
NCOEF = 25
KNB = 4
GHOST = 32
NRBF = 16
C = 128
OWN = 128
ROWS = NCOEF * C
WROWS = 115
TILES = KNB // 2
EDGES = TILES * OWN

EPSILON = 1e-06
SOFTENING = 0.25
STEP_TIME = 0.1
FRICTION = 0.9
RADIAL_SPREAD = 0.5

GROUPS = OWN // GHOST
PER_GROUP = -(-NCOEF // GROUPS)
PACKED = PER_GROUP * C
LAST = (NCOEF - (GROUPS - 1) * PER_GROUP) * C
GROUP_ROWS = (PACKED,) * (GROUPS - 1) + (LAST,)
GRANT = 18
STEP = 32
SHORT = 16

F32 = jnp.float32
BF16 = jnp.bfloat16


def frame_layout():
    layout = []
    offset = 0
    for degree in range(LMAX + 1):
        row_count = min(2 * degree + 1, 2 * MMAX + 1)
        layout.append((degree, row_count, offset))
        offset = offset + row_count * (2 * degree + 1)
    return layout


LAYOUT = frame_layout()
ORDER_START = (0, 5, 13)
EDGE_ROWS = 19


def edge_row(degree, row):
    if row == 0:
        return degree
    order = (row + 1) // 2
    return ORDER_START[order] + 2 * (degree - order) + (row + 1) % 2


def iota(shape, dim):
    return lax.broadcasted_iota(jnp.int32, shape, dim)


def dot(former, latter):
    return jnp.dot(former, latter, preferred_element_type=F32)


def one_hot(hit):
    return jnp.where(hit, 1.0, 0.0).astype(BF16)


def split_three(values):
    high = values.astype(BF16).astype(F32)
    rest = values - high
    middle = rest.astype(BF16).astype(F32)
    return high, middle, rest - middle


def side_bases():
    even = lax.rem(lax.axis_index("gx"), 2) == 0
    return jnp.where(even, OWN, 0), jnp.where(even, 0, OWN)


def rim_hits(atom, lane, group):
    low_base, high_base = side_bases()
    low = (lane - low_base - GHOST * group == atom) & (atom < GHOST)
    high = lane - high_base - GHOST * group == atom - (OWN - GHOST)
    return one_hot(low | (high & (atom >= OWN - GHOST)))


def rim_select(group):
    shape = (OWN, 2 * OWN)
    return rim_hits(iota(shape, 0), iota(shape, 1), group)


def rim_place(group):
    shape = (2 * OWN, OWN)
    return rim_hits(iota(shape, 1), iota(shape, 0), group)


def pack_rims(read_rows, low_ref, high_ref, extra=None):
    selects = [rim_select(group) for group in range(GROUPS)]
    for block in range(PER_GROUP):
        total = None
        for group in range(GROUPS):
            coef = PER_GROUP * group + block
            if coef < NCOEF:
                part = dot(read_rows(coef * C, C), selects[group])
                total = part if total is None else total + part
        low_ref[pl.ds(block * C, C), :] = total[:, :OWN].astype(BF16)
        high_ref[pl.ds(block * C, C), :] = total[:, OWN:].astype(BF16)
        if extra is not None and block * C == LAST:
            rows = extra.shape[0]
            total = total[:rows] + dot(extra, selects[GROUPS - 1])
            low_ref[pl.ds(block * C, rows), :] = total[:, :OWN].astype(BF16)
            high_ref[pl.ds(block * C, rows), :] = total[:, OWN:].astype(BF16)


def position_parts(pos_ref, parts_ref):
    parts_ref[...] = jnp.zeros_like(parts_ref)
    for at, part in enumerate(split_three(pos_ref[...])):
        parts_ref[pl.ds(8 * at, 3), :] = part
    return parts_ref[...].astype(BF16)


def fetch(pairs, sems):
    copies = [
        pltpu.make_async_copy(source, target, sems.at[at])
        for at, (source, target) in enumerate(pairs)
    ]
    for copy in copies:
        copy.start()
    for copy in copies:
        copy.wait()


def pack_kernel(feat_hbm, pos_hbm, low_ref, high_ref, feat_ref, pos_ref, parts_ref, sems):
    fetch([(feat_hbm, feat_ref), (pos_hbm, pos_ref)], sems)
    parts = position_parts(pos_ref, parts_ref)
    pack_rims(lambda start, size: feat_ref[pl.ds(start, size), :], low_ref, high_ref, parts)


INNER = 0
RIM = 1


def inside(shape, half):
    lane = iota(shape, 1)
    middle = (lane >= GHOST) & (lane < OWN - GHOST)
    return middle if half == INNER else jnp.logical_not(middle)


def pick(even, odd, half):
    return jnp.where(inside(even.shape, half), even, pltpu.roll(odd, OWN // 2, 1))


def both_lanes(values, half):
    return pick(values, values, half)


def fold_slots(values):
    return values + pltpu.roll(values, OWN // 2, 1)


def slot_rows(ref, half):
    tiles = []
    for tile in range(TILES):
        even = jnp.broadcast_to(ref[2 * tile : 2 * tile + 1, :], (8, OWN))
        odd = jnp.broadcast_to(ref[2 * tile + 1 : 2 * tile + 2, :], (8, OWN))
        tiles.append(pick(even, odd, half)[:1])
    return tiles


def edge_atoms(half):
    return both_lanes(iota((8, OWN), 1), half)[:1]


def edge_sources(nb_ref, half):
    own_at = []
    low_at = []
    high_at = []
    for rows in slot_rows(nb_ref, half):
        place = jnp.bitwise_and(rows, OWN - 1)
        gap = place - edge_atoms(half)
        low = gap > OWN // 2
        high = gap < -(OWN // 2)
        own_at.append(jnp.where(low | high, -1, place))
        low_at.append(jnp.where(low, place - (OWN - GHOST), -1))
        high_at.append(jnp.where(high, place, -1))
    merge = functools.partial(jnp.concatenate, axis=1)
    return merge(own_at), merge(low_at), merge(high_at)


def own_one_hot(own_at):
    return one_hot(iota((OWN, EDGES), 0) == own_at)


def ghost_one_hot(low_at, high_at, group):
    low_base, high_base = side_bases()
    at = jnp.where(high_at >= 0, high_at + (high_base + GHOST * group), -1)
    at = jnp.where(low_at >= 0, low_at + (low_base + GHOST * group), at)
    return one_hot(iota((2 * OWN, EDGES), 0) == at)


def half_frames(frames_ref, counts, half, wide_ref):
    total = KNB * OWN
    column = iota((total, EDGES), 1)
    lane = jnp.bitwise_and(column, OWN - 1)
    middle = (lane >= GHOST) & (lane < OWN - GHOST)
    held = middle if half == INNER else jnp.logical_not(middle)
    atom = jnp.where(held, lane, jnp.bitwise_and(lane + OWN // 2, OWN - 1))
    slot = 2 * (column // OWN) + jnp.where(held, 0, 1)
    moved = dot(frames_ref[...], one_hot(iota((total, EDGES), 0) == atom * KNB + slot))
    counts = both_lanes(jnp.broadcast_to(counts, (8, OWN)), half)[:1]
    odd = jnp.where(inside((1, OWN), half), 0, 1)
    live = jnp.concatenate(
        [jnp.where(2 * tile + odd < counts, 1.0, 0.0) for tile in range(TILES)], axis=1
    )
    moved = moved * live
    for entry in range(WROWS):
        wide_ref[entry] = jnp.broadcast_to(moved[entry : entry + 1, :], (8, EDGES))


def corner_mask(block):
    lane = jnp.bitwise_and(iota((C, 2 * OWN), 1), OWN - 1)
    return (lane < OWN - GHOST) | (block * C < LAST)


def read_ghosts(low_ref, high_ref, block):
    low = low_ref[pl.ds(block * C, C), :].astype(F32)
    high = high_ref[pl.ds(block * C, C), :].astype(F32)
    merged = jnp.concatenate([low, high], axis=1)
    if block * C >= LAST:
        merged = jnp.where(corner_mask(block), merged, 0.0)
    return merged


def fold_rows(values):
    return jnp.sum(values.reshape(-1, 8, values.shape[1]), axis=0)


def over_groups(values):
    column = jnp.broadcast_to(jnp.sum(values, axis=0, keepdims=True), values.shape)
    sides = []
    for side in range(2):
        part = column[:, side * OWN : (side + 1) * OWN]
        total = part
        for group in range(1, GROUPS):
            total = total + pltpu.roll(part, GHOST * group, 1)
        sides.append(total)
    return jnp.concatenate(sides, axis=1)[:1]


def normalise_own(feat_ref, own_ref):
    squares = jnp.zeros((8, OWN), F32)
    for coef in range(NCOEF):
        block = feat_ref[pl.ds(coef * C, C), :].astype(F32)
        squares = squares + fold_rows(block * block)
    mean = jnp.sum(squares, axis=0, keepdims=True) * (1.0 / ROWS)
    scale = lax.rsqrt(mean + EPSILON)
    for coef in range(NCOEF):
        rows = pl.ds(coef * C, C)
        own_ref[rows, :] = (feat_ref[rows, :].astype(F32) * scale).astype(BF16)
    return scale


def normalise_ghosts(low_ref, high_ref, ghost_ref):
    squares = jnp.zeros((8, 2 * OWN), F32)
    for block in range(PER_GROUP):
        values = read_ghosts(low_ref, high_ref, block)
        squares = squares + fold_rows(values * values)
    scale = lax.rsqrt(over_groups(squares) * (1.0 / ROWS) + EPSILON)
    for block in range(PER_GROUP):
        values = read_ghosts(low_ref, high_ref, block) * scale
        ghost_ref[pl.ds(block * C, C), :] = values.astype(BF16)
    return scale


def gather(own_ref, own_hot_ref, out_ref, ghost_ref=None, ghost_hot_ref=None):
    for group, rows in enumerate(GROUP_ROWS):
        start = group * PACKED
        found = dot(own_ref[pl.ds(start, rows), :], own_hot_ref[...])
        if ghost_ref is not None:
            found = found + dot(ghost_ref[pl.ds(0, rows), :], ghost_hot_ref[group])
        out_ref[pl.ds(start, rows), :] = found


def tall(values, rows):
    return jnp.concatenate([values] * (rows // 8), axis=0)


def slot_lanes(slot):
    return pl.ds(slot * OWN, OWN)


def to_frame(picked_ref, wide_ref, out_ref):
    @pl.loop(0, C // STEP)
    def _(step):
        start = pl.multiple_of(step * STEP, STEP)
        for slot in range(TILES):
            lanes = slot_lanes(slot)
            for degree, row_count, offset in LAYOUT:
                size = 2 * degree + 1
                parts = [
                    picked_ref[pl.ds((degree * degree + k) * C + start, STEP), lanes]
                    for k in range(size)
                ]
                for row in range(row_count):
                    total = None
                    for k in range(size):
                        term = tall(wide_ref[offset + row * size + k, :, lanes], STEP) * parts[k]
                        total = term if total is None else total + term
                    at = edge_row(degree, row) * C
                    out_ref[pl.ds(at + start, STEP), lanes] = total.astype(BF16)


def from_frame(frame_rows_ref, wide_ref, out_ref):
    @pl.loop(0, C // STEP)
    def _(step):
        start = pl.multiple_of(step * STEP, STEP)
        for slot in range(TILES):
            lanes = slot_lanes(slot)
            for degree, row_count, offset in LAYOUT:
                size = 2 * degree + 1
                parts = [
                    frame_rows_ref[pl.ds(edge_row(degree, row) * C + start, STEP), lanes]
                    for row in range(row_count)
                ]
                for k in range(size):
                    total = None
                    for row in range(row_count):
                        term = tall(wide_ref[offset + row * size + k, :, lanes], STEP) * parts[row]
                        total = term if total is None else total + term
                    at = (degree * degree + k) * C
                    out_ref[pl.ds(at + start, STEP), lanes] = total.astype(BF16)


def build_weights(weight_ref, layer, zero_ref, pair_ref):
    turned = [
        jnp.transpose(weight_ref[layer, part].astype(F32)).astype(BF16) for part in range(2 * MMAX + 1)
    ]
    zero_ref[...] = turned[0]
    for order in range(1, MMAX + 1):
        real, imag = turned[2 * order - 1], turned[2 * order]
        pair_ref[order - 1, :C, :C] = real
        pair_ref[order - 1, :C, C:] = -imag
        pair_ref[order - 1, C:, :C] = imag
        pair_ref[order - 1, C:, C:] = real


def build_back_weights(weight_ref, layer, zero_ref, pair_ref):
    zero_ref[...] = weight_ref[layer, 0]
    for order in range(1, MMAX + 1):
        real, imag = weight_ref[layer, 2 * order - 1], weight_ref[layer, 2 * order]
        pair_ref[order - 1, :C, :C] = real
        pair_ref[order - 1, :C, C:] = imag
        pair_ref[order - 1, C:, :C] = -imag
        pair_ref[order - 1, C:, C:] = real


def convolve(rows_ref, zero_ref, pair_ref, out_ref, keep_ref=None):
    def put(rows, found):
        out_ref[rows, :] = found
        if keep_ref is not None:
            keep_ref[rows, :] = found.astype(BF16)

    for degree in range(LMAX + 1):
        rows = pl.ds(degree * C, C)
        put(rows, dot(zero_ref[...], rows_ref[rows, :]))
    for order in range(1, MMAX + 1):
        for degree in range(order, LMAX + 1):
            rows = pl.ds((ORDER_START[order] + 2 * (degree - order)) * C, 2 * C)
            put(rows, dot(pair_ref[order - 1], rows_ref[rows, :]))


def radial(distance):
    centers = 0.5 + 5.5 * iota((NRBF, EDGES), 0).astype(F32) / (NRBF - 1)
    offset = (distance - centers) / RADIAL_SPREAD
    return jnp.exp(-(offset * offset)), offset


FORMER_PARTS = (0, 0, 1, 0, 2, 1)
LATTER_PARTS = (0, 1, 0, 2, 0, 1)


def stack_parts(values, order):
    parts = split_three(values)
    rest = C - len(order) * NRBF
    return jnp.concatenate(
        [parts[at] for at in order] + [jnp.zeros((rest, values.shape[1]), F32)], axis=0
    )


def gate_weights(radial):
    return jnp.transpose(stack_parts(radial * KNB ** (-0.5), FORMER_PARTS)).astype(BF16)


def edge_gate(gate_weight_ref, basis):
    return dot(gate_weight_ref[...], stack_parts(basis, LATTER_PARTS).astype(BF16))


def distance_slope(radial_ref, gate_slope, distance):
    basis, offset = radial(distance)
    basis_slope = jnp.dot(
        radial_ref[...], gate_slope, precision=lax.Precision.HIGHEST, preferred_element_type=F32
    )
    terms = basis_slope * basis * offset * (-2.0 * KNB ** (-0.5) / RADIAL_SPREAD)
    return jnp.sum(terms, axis=0, keepdims=True)


def message_rows(
    degree, row_count, offset, start, size_rows, turned_ref, gate_ref, wide_ref
):
    size = 2 * degree + 1
    sums = [None] * size
    for slot in range(TILES):
        lanes = slot_lanes(slot)
        gate = gate_ref[pl.ds(start, size_rows), lanes]
        for row in range(row_count):
            gated = turned_ref[pl.ds(edge_row(degree, row) * C + start, size_rows), lanes] * gate
            for k in range(size):
                term = tall(wide_ref[offset + row * size + k, :, lanes], size_rows) * gated
                sums[k] = term if sums[k] is None else sums[k] + term
    return [fold_slots(total) for total in sums]


def slope_rows(degree, offset, row, lanes, slopes, wide_ref):
    size = 2 * degree + 1
    size_rows = slopes[0].shape[0]
    total = None
    for k in range(size):
        term = tall(wide_ref[offset + row * size + k, :, lanes], size_rows) * slopes[k]
        total = term if total is None else total + term
    return total


def layer_forward(
    picked_ref, wide_ref, rows_ref, zero_ref, pair_ref, turned_ref, keep_ref=None
):
    to_frame(picked_ref, wide_ref, rows_ref)
    convolve(rows_ref, zero_ref, pair_ref, turned_ref, keep_ref)


def add_messages(base_ref, half, turned_ref, gate_ref, wide_ref, hidden_ref):
    @pl.loop(0, C // STEP, unroll=2)
    def _(step):
        start = pl.multiple_of(step * STEP, STEP)
        held = inside((STEP, OWN), half)
        for degree, row_count, offset in LAYOUT:
            sums = message_rows(
                degree, row_count, offset, start, STEP, turned_ref, gate_ref, wide_ref
            )
            for k, total in enumerate(sums):
                rows = pl.ds((degree * degree + k) * C + start, STEP)
                base = base_ref[rows, :].astype(F32)
                hidden_ref[rows, :] = jnp.where(held, base + total, base).astype(BF16)


def edge_geometry(source, shift, target, edge_ref):
    first = iota((8, EDGES), 0) == 0
    if shift is not None:
        source = source + jnp.where(first, shift, 0.0)
    vector = source - target
    distance = jnp.sqrt(jnp.sum(vector * vector, axis=0, keepdims=True) + SOFTENING)
    edge_ref[...] = jnp.where(iota((8, EDGES), 0) == 3, distance, vector)
    return distance


def join_parts(found):
    return (found[0:8] + found[8:16]) + found[16:24]


def first_inner_kernel(
    feat_hbm, frames_hbm, nb_hbm, counts_hbm, pos_hbm, box_hbm, weight_hbm, radial_hbm,
    readout_hbm, control_hbm,
    hidden_ref, keep_ref, edge_ref, own_ref, inner_wide_ref, rim_wide_ref, inner_hot_ref,
    rim_hot_ref, ghost_hot_ref, index_ref, target_ref, parts_out_ref, zero_ref, pair_ref,
    radial_ref, gate_weight_ref, readout_wide_ref, consts_ref,
    feat_ref, frames_ref, nb_ref, counts_ref, pos_ref, box_ref, weight_ref, readout_ref,
    control_ref,
    parts_ref, picked_ref, rows_ref, turned_ref, gate_ref, sems,
):
    fetch(
        [
            (nb_hbm, nb_ref), (counts_hbm, counts_ref), (pos_hbm, pos_ref),
            (box_hbm, box_ref), (frames_hbm, frames_ref), (radial_hbm, radial_ref),
            (feat_hbm, feat_ref), (weight_hbm, weight_ref), (readout_hbm, readout_ref),
            (control_hbm, control_ref),
        ],
        sems,
    )
    counts = counts_ref[...]
    half_frames(frames_ref, counts, INNER, inner_wide_ref)
    own_at, low_at, high_at = edge_sources(nb_ref, INNER)
    index_ref[...] = jnp.full((8, 2 * EDGES), -1, jnp.int32)
    index_ref[0:1, :EDGES] = own_at
    inner_hot_ref[...] = own_one_hot(own_at)
    parts = position_parts(pos_ref, parts_ref)
    parts_out_ref[...] = parts
    parts_ref[pl.ds(0, 3), :] = pos_ref[...]
    positions = parts_ref[0:8, :]
    target = jnp.concatenate([both_lanes(positions, INNER)] * TILES, axis=1)
    distance = edge_geometry(join_parts(dot(parts, inner_hot_ref[...])), None, target, edge_ref)
    for layer in range(2):
        gate_weight_ref[layer] = gate_weights(radial_ref[layer])
    gate_ref[...] = edge_gate(gate_weight_ref.at[0], radial(distance)[0])
    build_weights(weight_ref, 0, zero_ref.at[0], pair_ref.at[0])
    normalise_own(feat_ref, own_ref)
    gather(own_ref, inner_hot_ref, picked_ref)
    layer_forward(
        picked_ref, inner_wide_ref, rows_ref, zero_ref.at[0], pair_ref.at[0], turned_ref,
        keep_ref,
    )
    add_messages(feat_ref, INNER, turned_ref, gate_ref, inner_wide_ref, hidden_ref)
    row = iota((8, OWN), 0)
    consts = jnp.zeros((8, OWN), F32)
    for at in range(3):
        consts = jnp.where(row == at, box_ref[at], consts)
        consts = jnp.where(row == 3 + at, control_ref[at], consts)
    consts_ref[...] = consts
    half_frames(frames_ref, counts, RIM, rim_wide_ref)
    own_at, low_at, high_at = edge_sources(nb_ref, RIM)
    index_ref[0:1, EDGES:] = own_at
    index_ref[1:2, EDGES:] = low_at
    index_ref[2:3, EDGES:] = high_at
    rim_hot_ref[...] = own_one_hot(own_at)
    for group in range(GROUPS):
        ghost_hot_ref[group] = ghost_one_hot(low_at, high_at, group)
    place = lax.axis_index("gx")
    low_shift = jnp.where(place == 0, -box_ref[0], 0.0)
    high_shift = jnp.where(place == lax.axis_size("gx") - 1, box_ref[0], 0.0)
    shift = jnp.where(low_at >= 0, low_shift, jnp.where(high_at >= 0, high_shift, 0.0))
    target = jnp.concatenate([both_lanes(positions, RIM)] * TILES, axis=1)
    target_ref[...] = jnp.where(iota((8, EDGES), 0) == 3, shift, target)
    build_weights(weight_ref, 1, zero_ref.at[1], pair_ref.at[1])
    build_back_weights(weight_ref, 1, zero_ref.at[2], pair_ref.at[2])
    for degree in range(LMAX + 1):
        row = jnp.broadcast_to(readout_ref[degree : degree + 1, :], (C, C))
        readout_wide_ref[degree] = jnp.transpose(row) * (2.0 / (2 * degree + 1))


def first_rim_kernel(
    base_ref, low_ref, high_ref, own_ref, wide_ref, own_hot_ref, ghost_hot_ref, target_ref,
    parts_ref, zero_ref, pair_ref, gate_weight_ref,
    hidden_ref, keep_ref, edge_ref, send_low_ref, send_high_ref,
    ghost_ref, picked_ref, rows_ref, turned_ref, gate_ref,
):
    ghosts = jnp.concatenate(
        [low_ref[pl.ds(LAST, 32), :], high_ref[pl.ds(LAST, 32), :]], axis=1
    )
    found = dot(parts_ref[...], own_hot_ref[...]) + dot(ghosts, ghost_hot_ref[GROUPS - 1])
    target = jnp.where(iota((8, EDGES), 0) == 3, 0.0, target_ref[...])
    distance = edge_geometry(join_parts(found), target_ref[3:4, :], target, edge_ref)
    gate_ref[...] = edge_gate(gate_weight_ref.at[0], radial(distance)[0])
    normalise_ghosts(low_ref, high_ref, ghost_ref)
    gather(own_ref, own_hot_ref, picked_ref, ghost_ref, ghost_hot_ref)
    layer_forward(
        picked_ref, wide_ref, rows_ref, zero_ref.at[0], pair_ref.at[0], turned_ref, keep_ref
    )
    add_messages(base_ref, RIM, turned_ref, gate_ref, wide_ref, hidden_ref)
    pack_rims(lambda start, size: hidden_ref[pl.ds(start, size), :], send_low_ref, send_high_ref)


def turn_slopes(
    hidden_ref, half, turned_ref, gate_ref, wide_ref, readout_wide_ref, upper_ref,
    turned_slope_ref, gate_slope_ref,
):
    @pl.loop(0, C // SHORT)
    def _(step):
        start = pl.multiple_of(step * SHORT, SHORT)
        channels = pl.ds(start, SHORT)
        gate_slopes = [None] * TILES
        for degree, row_count, offset in LAYOUT:
            sums = message_rows(
                degree, row_count, offset, start, SHORT, turned_ref, gate_ref, wide_ref
            )
            weight = readout_wide_ref[degree, channels, :]
            slopes = []
            for k, total in enumerate(sums):
                rows = pl.ds((degree * degree + k) * C + start, SHORT)
                below = both_lanes(hidden_ref[rows, :].astype(F32), half)
                slope = (below + total) * weight
                upper_ref[rows, :] = slope
                slopes.append(slope)
            for slot in range(TILES):
                lanes = slot_lanes(slot)
                gate = gate_ref[channels, lanes]
                for row in range(row_count):
                    slope = slope_rows(
                        degree, offset, row, lanes, slopes, wide_ref
                    )
                    rows = pl.ds(edge_row(degree, row) * C + start, SHORT)
                    term = turned_ref[rows, lanes] * slope
                    before = gate_slopes[slot]
                    gate_slopes[slot] = term if before is None else before + term
                    turned_slope_ref[rows, lanes] = (slope * gate).astype(BF16)
        for slot in range(TILES):
            gate_slope_ref[channels, slot_lanes(slot)] = gate_slopes[slot]


def write_distance_slope(radial_ref, gate_slope_ref, distance, out_ref):
    slope = distance_slope(radial_ref, gate_slope_ref[...], distance)
    out_ref[...] = jnp.broadcast_to(slope, (8, EDGES))


def second_inner_kernel(
    hidden_ref, wide_ref, own_hot_ref, edge_ref, zero_ref, pair_ref, radial_ref, gate_weight_ref,
    readout_wide_ref,
    own_ref, scale_ref, upper_ref, turned_slope_ref, slope_ref,
    picked_ref, rows_ref, turned_ref, gate_ref, gate_slope_ref,
):
    distance = edge_ref[3:4, :]
    gate_ref[...] = edge_gate(gate_weight_ref.at[1], radial(distance)[0])
    scale_ref[...] = jnp.broadcast_to(normalise_own(hidden_ref, own_ref), (8, OWN))
    gather(own_ref, own_hot_ref, picked_ref)
    layer_forward(picked_ref, wide_ref, rows_ref, zero_ref.at[1], pair_ref.at[1], turned_ref)
    turn_slopes(
        hidden_ref, INNER, turned_ref, gate_ref, wide_ref, readout_wide_ref, upper_ref,
        turned_slope_ref, gate_slope_ref,
    )
    write_distance_slope(radial_ref.at[1], gate_slope_ref, distance, slope_ref)


def scatter_own(edge_slope_ref, own_hot_ref, out_ref, add_ref=None):
    spread = jnp.transpose(own_hot_ref[...].astype(F32)).astype(BF16)
    for group, rows in enumerate(GROUP_ROWS):
        block = pl.ds(group * PACKED, rows)
        part = dot(edge_slope_ref[block, :], spread)
        out_ref[block, :] = part if add_ref is None else part + add_ref[block, :]


def second_rim_kernel(
    hidden_ref, low_ref, high_ref, own_ref, wide_ref, own_hot_ref, ghost_hot_ref, edge_ref,
    zero_ref, pair_ref, radial_ref, gate_weight_ref, readout_wide_ref,
    upper_ref, slope_ref, own_slope_ref, send_low_ref, send_high_ref,
    ghost_ref, picked_ref, rows_ref, turned_ref, gate_ref, gate_slope_ref, turned_slope_ref,
    edge_slope_ref, ghost_slope_ref,
):
    distance = edge_ref[3:4, :]
    gate_ref[...] = edge_gate(gate_weight_ref.at[1], radial(distance)[0])
    ghost_scale = normalise_ghosts(low_ref, high_ref, ghost_ref)
    gather(own_ref, own_hot_ref, picked_ref, ghost_ref, ghost_hot_ref)
    layer_forward(picked_ref, wide_ref, rows_ref, zero_ref.at[1], pair_ref.at[1], turned_ref)
    turn_slopes(
        hidden_ref, RIM, turned_ref, gate_ref, wide_ref, readout_wide_ref, upper_ref,
        turned_slope_ref, gate_slope_ref,
    )
    convolve(turned_slope_ref, zero_ref.at[2], pair_ref.at[2], turned_ref)
    from_frame(turned_ref, wide_ref, edge_slope_ref)
    for group, rows in enumerate(GROUP_ROWS):
        spread_ghost = jnp.transpose(ghost_hot_ref[group].astype(F32)).astype(BF16)
        part = dot(edge_slope_ref[pl.ds(group * PACKED, rows), :], spread_ghost)
        if group == 0:
            ghost_slope_ref[...] = part
        else:
            ghost_slope_ref[pl.ds(0, rows), :] += part
    along = jnp.zeros((8, 2 * OWN), F32)
    for block in range(PER_GROUP):
        values = read_ghosts(low_ref, high_ref, block)
        along = along + fold_rows(ghost_slope_ref[pl.ds(block * C, C), :] * values)
    along = over_groups(along) * (1.0 / ROWS)
    along = along * ghost_scale * ghost_scale * ghost_scale
    for block in range(PER_GROUP):
        rows = pl.ds(block * C, C)
        values = read_ghosts(low_ref, high_ref, block)
        back = ghost_slope_ref[rows, :] * ghost_scale - values * along
        send_low_ref[rows, :] = back[:, :OWN].astype(BF16)
        send_high_ref[rows, :] = back[:, OWN:].astype(BF16)
    scatter_own(edge_slope_ref, own_hot_ref, own_slope_ref)
    write_distance_slope(radial_ref.at[1], gate_slope_ref, distance, slope_ref)


def gate_slopes_back(hidden_slope_ref, half, wide_ref, keep_ref, gate_slope_ref):
    @pl.loop(0, C // STEP, unroll=2)
    def _(step):
        start = pl.multiple_of(step * STEP, STEP)
        gate_slopes = [None] * TILES
        for degree, row_count, offset in LAYOUT:
            slopes = [
                both_lanes(
                    hidden_slope_ref[pl.ds((degree * degree + k) * C + start, STEP), :], half
                )
                for k in range(2 * degree + 1)
            ]
            for slot in range(TILES):
                lanes = slot_lanes(slot)
                for row in range(row_count):
                    slope = slope_rows(
                        degree, offset, row, lanes, slopes, wide_ref
                    )
                    rows = pl.ds(edge_row(degree, row) * C + start, STEP)
                    term = keep_ref[rows, lanes].astype(F32) * slope
                    before = gate_slopes[slot]
                    gate_slopes[slot] = term if before is None else before + term
        for slot in range(TILES):
            gate_slope_ref[pl.ds(start, STEP), slot_lanes(slot)] = gate_slopes[slot]


def edge_pulls(radial_ref, gate_slope_ref, edge_ref, second_slope_ref, half):
    distance = edge_ref[3:4, :]
    slope = distance_slope(radial_ref, gate_slope_ref[...], distance) + second_slope_ref[0:1, :]
    vector = jnp.where(iota((8, EDGES), 0) < 3, edge_ref[...], 0.0)
    pull = vector * (slope / distance)
    virial = -jnp.sum(pull * vector)
    high, middle, low = split_three(pull)
    parts = jnp.concatenate([high, middle, low, jnp.zeros((8, EDGES), F32)], axis=0).astype(BF16)
    on_target = pull[:, :OWN]
    for tile in range(1, TILES):
        on_target = on_target + pull[:, tile * OWN : (tile + 1) * OWN]
    on_target = jnp.where(inside((8, OWN), half), fold_slots(on_target), 0.0)
    return parts, on_target, virial


def spread(hot):
    return jnp.transpose(hot.astype(F32)).astype(BF16)


def middle_kernel(
    hidden_ref, scale_ref, inner_upper_ref, rim_upper_ref, own_slope_ref, turned_slope_ref,
    wide_ref, own_hot_ref, zero_ref, pair_ref, radial_ref, keep_ref, edge_ref,
    second_slope_ref,
    slope_ref, part_ref,
    turned_ref, edge_slope_ref, gate_slope_ref,
):
    convolve(turned_slope_ref, zero_ref.at[2], pair_ref.at[2], turned_ref)
    from_frame(turned_ref, wide_ref, edge_slope_ref)
    scatter_own(edge_slope_ref, own_hot_ref, slope_ref, own_slope_ref)
    scale = scale_ref[0:1, :]
    along = jnp.zeros((8, OWN), F32)
    for coef in range(NCOEF):
        rows = pl.ds(coef * C, C)
        along = along + fold_rows(slope_ref[rows, :] * hidden_ref[rows, :].astype(F32))
    along = jnp.sum(along, axis=0, keepdims=True) * (1.0 / ROWS)
    along = along * scale * scale * scale
    held = inside((C, OWN), INNER)
    for coef in range(NCOEF):
        rows = pl.ds(coef * C, C)
        upper = jnp.where(held, inner_upper_ref[rows, :], rim_upper_ref[rows, :])
        total = upper + slope_ref[rows, :] * scale - hidden_ref[rows, :].astype(F32) * along
        slope_ref[rows, :] = total
    gate_slopes_back(slope_ref, INNER, wide_ref, keep_ref, gate_slope_ref)
    parts, on_target, virial = edge_pulls(
        radial_ref.at[0], gate_slope_ref, edge_ref, second_slope_ref, INNER
    )
    landed = join_parts(dot(parts, spread(own_hot_ref[...]))) - on_target
    part_ref[...] = jnp.where(iota((8, OWN), 0) == 7, virial, landed)


def last_kernel(
    slope_ref, low_ref, high_ref, wide_ref, own_hot_ref, index_ref, radial_ref, keep_ref,
    edge_ref, second_slope_ref, part_ref, velocities_ref, masses_ref,
    tile_ref,
    gate_slope_ref, hidden_slope_ref,
):
    for group, rows in enumerate(GROUP_ROWS):
        block = pl.ds(group * PACKED, rows)
        back = jnp.concatenate([low_ref[pl.ds(0, rows), :], high_ref[pl.ds(0, rows), :]], axis=1)
        hidden_slope_ref[block, :] = slope_ref[block, :] + dot(back, rim_place(group))
    gate_slopes_back(hidden_slope_ref, RIM, wide_ref, keep_ref, gate_slope_ref)
    parts, on_target, virial = edge_pulls(
        radial_ref.at[0], gate_slope_ref, edge_ref, second_slope_ref, RIM
    )
    landed = join_parts(dot(parts, spread(own_hot_ref[...]))) - on_target + part_ref[...]
    low_at, high_at = index_ref[1:2, EDGES:], index_ref[2:3, EDGES:]
    rim_at = jnp.where(low_at >= 0, low_at + (OWN - GHOST), high_at)
    outward = -join_parts(dot(parts, spread(own_one_hot(rim_at))))
    virial = virial + part_ref[7:8, :]
    masses = masses_ref[...]
    speed = jnp.concatenate([velocities_ref[...], jnp.zeros((5, OWN), F32)], axis=0)
    per_mass = STEP_TIME / masses
    kicked = speed - landed * per_mass
    lane = iota((8, OWN), 1)
    row = iota((8, OWN), 0)
    inner = (row < 3) & (lane >= GHOST) & (lane < OWN - GHOST)
    strain = virial + jnp.sum(jnp.where(inner, masses * kicked * kicked, 0.0))
    tile = jnp.where(row < 3, kicked, jnp.where(row == 3, per_mass, pltpu.roll(outward, 4, 0)))
    tile_ref[...] = jnp.where(row == 7, strain, tile)


def join_tiles(left, right):
    lane = iota((8, OWN), 1)
    row = iota((8, OWN), 0)
    top = lane >= OWN - GHOST
    rims = top | (lane < GHOST)
    near = jnp.where(top, left, right)
    pushed = pltpu.roll(jnp.where(top, right, left), 4, 0)
    per_mass = near[3:4]
    kicked = near + per_mass * pushed
    terms = jnp.where(rims & (row < 3), kicked * kicked * (STEP_TIME / per_mass), 0.0)
    return jnp.sum(terms)


def merge_runs(width, ways, tiles, caught):
    place = lax.axis_index("gx")
    lane = iota((8, OWN), 1)
    row = iota((8, OWN), 0)
    top = lane >= OWN - GHOST
    bottom = lane < GHOST
    digit = lax.rem(place // width, ways)
    at_start = lax.rem(place, width) == 0
    at_end = lax.rem(place, width) == width - 1
    ordered = []
    for run in range(ways):
        chosen = tiles[0]
        step = digit ^ run if ways in (2, 4) else lax.rem(run - digit + ways, ways)
        for far in range(1, ways):
            chosen = jnp.where(step == far, tiles[far], chosen)
        ordered.append(chosen)
    merged = ordered[0]
    for run in range(1, ways):
        right = ordered[run]
        caught = jnp.where(top & (at_end & (digit == run - 1)), right, caught)
        caught = jnp.where(bottom & (at_start & (digit == run)), merged, caught)
        strain = merged + right + join_tiles(merged, right)
        outer = jnp.where(top == (row < 4), right, merged)
        merged = jnp.where(row == 7, strain, outer)
    return merged, caught


def merge_kernel(width, ways, *refs):
    ins, (tile_ref, caught_ref) = refs[:-2], refs[-2:]
    tiles = [ref[...] for ref in ins[:ways]]
    caught = ins[ways][...] if len(ins) > ways else jnp.zeros((8, OWN), F32)
    tile_ref[...], caught_ref[...] = merge_runs(width, ways, tiles, caught)


def finish_kernel(width, ways, first_round, *refs):
    (
        masses_ref, noise_ref, positions_ref, consts_ref,
        fractional_ref, velocities_ref, new_box_ref,
    ) = refs[-7:]
    tiles = [ref[...] for ref in refs[:ways]]
    start = tiles[0] if first_round else refs[ways][...]
    caught = jnp.zeros((8, OWN), F32) if first_round else refs[ways + 1][...]
    merged, caught = merge_runs(width, ways, tiles, caught)
    place = lax.axis_index("gx")
    lane = iota((8, OWN), 1)
    caught = jnp.where((lane >= OWN - GHOST) & (place == width * ways - 1), merged, caught)
    caught = jnp.where((lane < GHOST) & (place == 0), merged, caught)
    strain = merged[7:8] + join_tiles(merged, merged)
    kicked = (start + start[3:4] * pltpu.roll(caught, 4, 0))[0:3]
    box = consts_ref[0:3, :]
    temperature, coupling, wanted = (consts_ref[at : at + 1, :] for at in (3, 4, 5))
    volume = consts_ref[0:1, :] * consts_ref[1:2, :] * consts_ref[2:3, :]
    pressure = strain / (3.0 * volume)
    rescale = jnp.exp(coupling * (pressure - wanted) / 3.0)
    kick = jnp.sqrt((1.0 - FRICTION * FRICTION) * temperature / masses_ref[...])
    thermal = FRICTION * kicked + kick * noise_ref[...]
    fractional_ref[...] = (positions_ref[...] + STEP_TIME * thermal) / box
    velocities_ref[...] = thermal / rescale
    scaled = box * rescale
    for side in range(3):
        new_box_ref[side] = scaled[side, 0]


def call(kernel, outs, scratch, args, grant=GRANT, hbm=False, cost=1):
    space = pltpu.HBM if hbm else pltpu.VMEM

    def buffer(entry):
        return entry if len(entry) == 3 else entry + (pltpu.VMEM,)

    buffers = []
    for entry in scratch:
        if isinstance(entry, int):
            buffers.append(pltpu.SemaphoreType.DMA((entry,)))
        else:
            shape, kind, where = buffer(entry)
            buffers.append(where(shape, kind))
    return pl.pallas_call(
        kernel,
        out_shape=[jax.ShapeDtypeStruct(shape, kind) for shape, kind in outs],
        in_specs=[pl.BlockSpec(memory_space=space) for _ in args],
        out_specs=[
            pl.BlockSpec(memory_space=pltpu.SMEM if len(shape) == 1 else pltpu.VMEM)
            for shape, kind in outs
        ],
        scratch_shapes=buffers,
        compiler_params=pltpu.CompilerParams(vmem_limit_bytes=grant << 20),
        cost_estimate=pl.CostEstimate(
            flops=cost << 30, bytes_accessed=1 << 20, transcendentals=0
        ),
    )(*args.values())


def shards(
    node_feat,
    frames,
    neighbours,
    counts,
    positions,
    velocities,
    masses,
    thermal_noise,
    box_lengths,
    control,
    conv_weight,
    radial_weight,
    readout,
):
    assert positions.shape[1] == OWN
    count = lax.axis_size("gx")
    assert count % 2 == 0
    within = [(i, i ^ 1) for i in range(count)]
    across = [(i, (i + 2 * (i % 2) - 1) % count) for i in range(count)]

    def exchange(to_first, to_second):
        from_second = lax.ppermute(to_second, "gx", across)
        from_first = lax.ppermute(to_first, "gx", within)
        return from_first, from_second

    packed = ((PACKED, OWN), BF16)
    own_rows = ((ROWS, OWN), BF16)
    own_sums = ((ROWS, OWN), F32)
    kept = ((EDGE_ROWS * C, EDGES), BF16)
    turned = ((EDGE_ROWS * C, EDGES), F32)
    picked = ((ROWS, EDGES), F32)
    edge = ((8, EDGES), F32)
    wide = ((WROWS, 8, EDGES), F32)
    gate = ((C, EDGES), F32)
    hot = ((OWN, EDGES), BF16)
    ghost = ((PACKED, 2 * OWN), BF16)
    small = ((8, OWN), F32)
    place = ((3, OWN), F32)
    parts = ((32, OWN), F32)
    mass_row = masses[None, :]
    to_low, to_high = call(
        pack_kernel,
        [packed, packed],
        [own_rows, place, parts, 2],
        dict(feat=node_feat, positions=positions),
        grant=8,
        hbm=True,
    )
    from_low, from_high = exchange(to_low, to_high)
    (
        hidden, keep_inner, edge_inner, own, wide_inner, wide_rim, hot_inner, hot_rim,
        hot_ghost, index, target, own_parts, zero, pair, radial_rows, gate_weight,
        readout_wide, consts,
    ) = call(
        first_inner_kernel,
        [
            own_rows, kept, edge, own_rows, wide, wide, hot, hot,
            ((GROUPS, 2 * OWN, EDGES), BF16), ((8, 2 * EDGES), jnp.int32), edge,
            ((32, OWN), BF16), ((3, C, C), BF16), ((3, MMAX, 2 * C, 2 * C), BF16),
            (radial_weight.shape, F32), ((2, C, C), BF16), ((LMAX + 1, C, C), F32), small,
        ],
        [
            own_rows, (frames.shape, BF16), ((KNB, OWN), jnp.int32), ((1, OWN), jnp.int32),
            place, ((3,), F32, pltpu.SMEM), (conv_weight.shape, BF16), (readout.shape, F32),
            ((3,), F32, pltpu.SMEM), parts, picked, kept, turned, gate, 10,
        ],
        dict(
            feat=node_feat, frames=frames, neighbours=neighbours, counts=counts[None, :],
            positions=positions, box=box_lengths, weight=conv_weight, radial=radial_weight,
            readout=readout, control=control,
        ),
        hbm=True,
        cost=5,
    )
    hidden, keep_rim, edge_rim, to_low, to_high = call(
        first_rim_kernel,
        [own_rows, kept, edge, packed, packed],
        [ghost, picked, kept, turned, gate],
        dict(
            base=hidden, low=from_low, high=from_high, own=own, wide=wide_rim, hot=hot_rim,
            ghost_hot=hot_ghost, target=target, parts=own_parts, zero=zero, pair=pair,
            gate_weight=gate_weight,
        ),
    )
    from_low, from_high = exchange(to_low, to_high)
    own, scale, upper_inner, turned_slope, slope_inner = call(
        second_inner_kernel,
        [own_rows, small, own_sums, kept, edge],
        [picked, kept, turned, gate, gate],
        dict(
            hidden=hidden, wide=wide_inner, hot=hot_inner, edge=edge_inner, zero=zero,
            pair=pair, radial=radial_rows, gate_weight=gate_weight, readout=readout_wide,
        ),
        cost=5,
    )
    upper_rim, slope_rim, own_slope, to_low, to_high = call(
        second_rim_kernel,
        [own_sums, edge, own_sums, packed, packed],
        [
            ghost, picked, kept, turned, gate, gate, kept, ((ROWS, EDGES), BF16),
            ((PACKED, 2 * OWN), F32),
        ],
        dict(
            hidden=hidden, low=from_low, high=from_high, own=own, wide=wide_rim, hot=hot_rim,
            ghost_hot=hot_ghost, edge=edge_rim, zero=zero, pair=pair, radial=radial_rows,
            gate_weight=gate_weight, readout=readout_wide,
        ),
    )
    from_low, from_high = exchange(to_low, to_high)
    slope, part = call(
        middle_kernel,
        [own_sums, small],
        [turned, ((ROWS, EDGES), BF16), gate],
        dict(
            hidden=hidden, scale=scale, upper_inner=upper_inner, upper_rim=upper_rim,
            own_slope=own_slope, turned_slope=turned_slope, wide=wide_inner, hot=hot_inner,
            zero=zero, pair=pair, radial=radial_rows, keep=keep_inner, edge=edge_inner,
            second_slope=slope_inner,
        ),
        cost=5,
    )
    (tile,) = call(
        last_kernel,
        [small],
        [gate, own_sums],
        dict(
            slope=slope, low=from_low, high=from_high, wide=wide_rim, hot=hot_rim, index=index,
            radial=radial_rows, keep=keep_rim, edge=edge_rim, second_slope=slope_rim,
            part=part, velocities=velocities, masses=mass_row,
        ),
    )
    own = tile
    caught = None
    width = 1
    while True:
        left = count // width
        ways = next(way for way in (4, 2, 3, left) if left % way == 0)
        tiles = {"tile0": tile}
        for far in range(1, ways):
            pairs = []
            for target in range(count):
                digit = target // width % ways
                other = digit ^ far if ways in (2, 4) else (digit + far) % ways
                source = target + (other - digit) * width
                pairs.append((source, target))
            tiles["tile%d" % far] = lax.ppermute(tile, "gx", pairs)
        if caught is not None:
            tiles["caught"] = caught
        if width * ways == count:
            break
        tile, caught = call(
            functools.partial(merge_kernel, width, ways), [small, small], [], tiles, grant=1
        )
        width = width * ways
    if caught is not None:
        del tiles["caught"]
        tiles.update(own=own, caught=caught)
    return call(
        functools.partial(finish_kernel, width, ways, caught is None),
        [((3, OWN), F32), ((3, OWN), F32), ((3,), F32)],
        [],
        dict(
            tiles, masses=mass_row, noise=thermal_noise, positions=positions,
            consts=consts,
        ),
        grant=1,
    )


def solution(mesh):
    return jax.shard_map(
        shards,
        mesh=mesh,
        in_specs=(
            P(None, ("groups", "gx")),
            P(None, ("groups", "gx")),
            P(None, ("groups", "gx")),
            P(("groups", "gx")),
            P(None, ("groups", "gx")),
            P(None, ("groups", "gx")),
            P(("groups", "gx")),
            P(None, ("groups", "gx")),
            P("groups"),
            P("groups"),
            P(),
            P(),
            P(),
        ),
        out_specs=(P(None, ("groups", "gx")), P(None, ("groups", "gx")), P("groups")),
        check_vma=False,
    )
```
